128 devices in a mesh: ang: 32 (over y, x, core), grp: 4 (over z).
Axes of the slice: x: 4, y: 4, z: 4, core: 2. Of those that a mesh axis runs over, the one named last changes fastest.
Arguments:
- phases: float32 [32, 1024, 1024], P('ang'), may hold values from -6 to 6
- holograms: bfloat16 [4, 32, 1024, 1024], P('grp', 'ang'), may hold values from -6 to 6
- ctf_phase: float32 [4], replicated, may hold values from 50 to 400
- projected: float32 [32, 1024, 1024], P('ang', None, 'grp'), may hold values from -6 to 6
- multiplier: float32 [32, 1024, 1024], P('ang', None, 'grp'), may hold values from -3 to 3
- volume: float32 [128, 1024, 1024], P('ang', None, 'grp'), may hold values from -1.5 to 1.5
- band_length: int32 [32], replicated, may hold values from 1 to 64, 1024 in all
- line_rows: int32 [32, 128, 64], P(None, 'ang'), may hold values from 0 to 63
Outputs:
- new_phases: float32 [32, 1024, 1024], P('ang', None, 'grp')
- new_volume: float32 [128, 1024, 1024], P('ang', None, 'grp')
- new_multiplier: float32 [32, 1024, 1024], P('ang', None, 'grp')
The draws below stay inside these ranges and needn't reach their ends.
Inputs may be any that keep to these rules, and one draw needn't show every extreme that they name: `band_length`: the lengths sum to 1024; one of them equals 64.
All inputs are finite; a program needn't handle non-finite values.
Results may differ from the reference program's by a relative error of at most 0.015.
The reference program's roundings to bfloat16 on the way (of `resid`) count: a program that leaves them out, or rounds other values in their place, can miss the bound.
Values sent between devices are 32-bit elements; how exact they have to be, the bound alone decides.
A program may use at most 128 MiB of HBM per device.

```python
import math
import jax
import jax.numpy as jnp
import numpy as np
from jax import lax

ROWS = 1024
COLS = 1024
DIST = 4
SLAB_Z = 4
DEPTH = 1024
YBLOCK = 16
ANGLES = 32
NZ = 128
NBLOCK = 64
BAND = 64
SLABS = 32


def with_ends(values, rng, low, high):
    longest = values.shape.index(max(values.shape))
    spots = []
    for shift in (0, 1):
        where = [jax.random.randint(jax.random.fold_in(rng, axis), (), 0, length) for axis, length in enumerate(values.shape)]
        where[longest] = (where[longest] + shift) % values.shape[longest]
        spots.append(tuple(where))
    return values.at[spots[0]].set(low).at[spots[1]].set(high)


def shard_levels(key, extent, cuts, low, top_value):
    level, own = 1.0, jax.random.fold_in(key, 6)
    for dim, shards_of in cuts:
        steps = jnp.exp(jax.random.uniform(jax.random.fold_in(own, dim), (shards_of,), jnp.float32, low / len(cuts), top_value / len(cuts)))
        level = level * jnp.repeat(steps, extent[dim] // shards_of).reshape([-1 if axis == dim else 1 for axis in range(len(extent))])
    return level


def length_profile(amount, total, reach, slope):
    loads = [(1 << 20) // math.isqrt(standing ** slope) + 1 for standing in range(2, amount + 1)]
    spare, counts = total - reach - (amount - 1), [1] * (amount - 1)
    while spare > 0:
        movable = [i for i in range(amount - 1) if counts[i] < reach]
        mass, remaining = sum([loads[i] for i in movable]), spare
        for i in movable:
            extra = min(reach - counts[i], max(1, remaining * loads[i] // mass), spare)
            counts[i] = counts[i] + extra
            spare = spare - extra
    return np.array([reach] + counts)


def ragged(stream_key, number_of, total, bound, slope):
    if number_of == 2:
        one = jax.random.randint(stream_key, (), max(1, total - bound), min(bound, total - 1) + 1)
        return jnp.stack([one, total - one])
    sizes = jnp.asarray(length_profile(number_of, total, bound, slope), jnp.int32)
    couples = (number_of - 1) // 2
    source_of, sink = sizes[1:1 + 2 * couples:2], sizes[2:2 + 2 * couples:2]
    margin = jnp.minimum(source_of - 1, bound - sink)
    passed = jax.random.randint(jax.random.fold_in(stream_key, 1), (couples,), 0, 1 << 20) % (margin + 1)
    sizes = sizes.at[1:1 + 2 * couples:2].set(source_of - passed).at[2:2 + 2 * couples:2].set(sink + passed)
    return sizes[jax.random.permutation(jax.random.fold_in(stream_key, 2), number_of)]


def noise(stream_key, extent, scale, reach, pieces=(), held_as=jnp.bfloat16):
    gain = shard_levels(stream_key, extent, pieces, -0.22, 0.18) if pieces else 1.0
    array = jax.random.normal(stream_key, extent, jnp.float32) * scale * gain
    return jnp.minimum(jnp.maximum(array, -reach), reach).astype(held_as)


def setup_inputs(seed: int = 0) -> dict:
    splits = jax.random.split(jax.random.key(seed), 9)
    phases = noise(splits[0], (ANGLES, ROWS, COLS), 1.0, 6.0, ((0, 32),), jnp.float32)
    holograms = noise(splits[1], (DIST, ANGLES, ROWS, COLS), 1.0, 6.0, ((0, 4), (1, 32)))
    ctf_phase = jnp.clip(jnp.exp(jax.random.uniform(splits[2], (DIST,), jnp.float32, math.log(50.0), math.log(400.0))), 50.0, 400.0)
    projected = noise(splits[3], (ANGLES, ROWS, COLS), 1.0, 6.0, ((0, 32), (2, 4)), jnp.float32)
    multiplier = noise(splits[4], (ANGLES, ROWS, COLS), 0.5, 3.0, ((0, 32), (2, 4)), jnp.float32)
    volume = noise(splits[5], (NZ, DEPTH, COLS), 0.25, 1.5, ((0, 32), (2, 4)), jnp.float32)
    band_length = ragged(splits[6], SLABS, ROWS, BAND, 2).astype(jnp.int32)
    line_rows = with_ends(jax.random.randint(splits[7], (ANGLES, NZ, NBLOCK), 0, BAND), jax.random.fold_in(splits[7], 1), 0, BAND - 1).astype(jnp.int32)
    return dict(phases=phases, holograms=holograms, ctf_phase=ctf_phase, projected=projected, multiplier=multiplier, volume=volume, band_length=band_length, line_rows=line_rows)


step_phase = 0.2
penalty = 0.5
step_volume = 0.004


def cas_table(length):
    places = jnp.arange(length, dtype=jnp.int32)
    product = (places[:, None] * places[None, :]) % length
    angle = product.astype(jnp.float32) * (2.0 * math.pi / length)
    return (jnp.cos(angle) + jnp.sin(angle)).astype(jnp.bfloat16)


def freq_square(length):
    places = jnp.arange(length, dtype=jnp.int32)
    folded = jnp.minimum(places, length - places).astype(jnp.float32) / length
    return folded * folded


def ctf_weight(coefficient, rows, cols):
    radius = freq_square(rows)[:, None] + freq_square(cols)[None, :]
    return 2.0 * jnp.sin(coefficient * radius) / (rows * cols)


def propagate(image, weight, row_table, col_table):
    first = jnp.dot(image, col_table, preferred_element_type=jnp.float32).astype(jnp.bfloat16)
    spectrum = jnp.dot(row_table, first, preferred_element_type=jnp.float32)
    filtered = (weight * spectrum).astype(jnp.bfloat16)
    back = jnp.dot(row_table, filtered, preferred_element_type=jnp.float32).astype(jnp.bfloat16)
    return jnp.dot(back, col_table, preferred_element_type=jnp.float32)


def block_sums(slab_volume):
    depth_rows, depth, width = slab_volume.shape
    grouped = slab_volume.reshape(depth_rows, depth // YBLOCK, YBLOCK, width)
    return jnp.sum(grouped, axis=2).reshape(depth_rows * (depth // YBLOCK), width)


def spread(update, shape):
    depth_rows, depth, width = shape
    shaped = update.reshape(depth_rows, depth // YBLOCK, 1, width)
    return jnp.broadcast_to(shaped, (depth_rows, depth // YBLOCK, YBLOCK, width)).reshape(shape)


def reference(phases, holograms, ctf_phase, projected, multiplier, volume, band_length, line_rows):
    row_table = cas_table(ROWS)
    col_table = cas_table(COLS)
    weights = [ctf_weight(ctf_phase[dist], ROWS, COLS) for dist in range(DIST)]

    def one_angle(packed):
        image, shots = packed
        total = jnp.zeros((ROWS, COLS), jnp.float32)
        for dist in range(DIST):
            model = propagate(image.astype(jnp.bfloat16), weights[dist], row_table, col_table)
            resid = (model - shots[dist].astype(jnp.float32)).astype(jnp.bfloat16)
            term = propagate(resid, weights[dist], row_table, col_table)
            total = total + term
        return total

    gradient = lax.map(one_angle, (phases, jnp.moveaxis(holograms, 0, 1)))
    new_phases = phases - step_phase * (gradient + penalty * (phases - projected) + multiplier)
    target = new_phases + multiplier / penalty

    lengths = band_length.astype(jnp.int32)
    ends = jnp.cumsum(lengths).astype(jnp.int32)
    starts = (ends - lengths).astype(jnp.int32)
    offsets = jnp.arange(BAND, dtype=jnp.int32)
    sources = jnp.clip(starts[:, None] + offsets[None, :], 0, ROWS - 1).astype(jnp.int32)
    valid = (offsets[None, :] < lengths[:, None]).astype(jnp.float32)
    band_target = jnp.take(target, sources.reshape(-1), axis=1).reshape(ANGLES, SLABS, BAND, COLS)
    band_target = jnp.moveaxis(band_target * valid[None, :, :, None], 1, 0)

    slab_volume = volume.reshape(SLABS, SLAB_Z, DEPTH, COLS)
    slab_lines = jnp.moveaxis(line_rows.reshape(ANGLES, SLABS, SLAB_Z * NBLOCK), 1, 0)

    def one_slab(packed):
        part_volume, lines, rows_target, own_length = packed
        hits = (lines[:, None, :] == offsets[None, :, None]) & (offsets[None, :, None] < own_length)
        hits = hits.astype(jnp.float32)
        image = jnp.einsum('akm,mc->akc', hits, block_sums(part_volume), precision=lax.Precision.HIGHEST)
        misfit = image - rows_target
        update = jnp.einsum('akm,akc->mc', hits, misfit, precision=lax.Precision.HIGHEST)
        fresh = part_volume - step_volume * spread(update, part_volume.shape)
        again = jnp.einsum('akm,mc->akc', hits, block_sums(fresh), precision=lax.Precision.HIGHEST)
        return fresh, again

    fresh_slabs, new_proj = lax.map(one_slab, (slab_volume, slab_lines, band_target, lengths))
    new_volume = fresh_slabs.reshape(NZ, DEPTH, COLS)
    positions = jnp.arange(ROWS, dtype=jnp.int32)
    owner = jnp.sum((ends[None, :] <= positions[:, None]).astype(jnp.int32), axis=1).astype(jnp.int32)
    within = (positions - starts[owner]).astype(jnp.int32)
    model_rows = jnp.transpose(new_proj[owner, :, within, :], (1, 0, 2))
    new_multiplier = multiplier + penalty * (new_phases - model_rows)
    return new_phases, new_volume, new_multiplier
```

```python
import functools

import jax
import jax.numpy as jnp
import ml_dtypes
import numpy as np
from jax import lax
from jax.experimental import pallas as pl
from jax.experimental.pallas import tpu as pltpu
from jax.sharding import PartitionSpec as P

f32 = jnp.float32
bf16 = jnp.bfloat16
MESH = pl.DeviceIdType.MESH

N = 1024
QUARTER = 256
CHUNK = 128
CHUNKS = 2
SLABS = 32
BAND = 64
LINES = 256
GROUPS = 4
HALF = N // 2
PAD = N + BAND
OPP, OWN, UP, DN = range(4)

step_phase = 0.2
penalty = 0.5
step_volume = 0.004
YBLOCK = 16


def cas_table():
    places = np.arange(N)
    angle = (places[:, None] * places[None, :] % N).astype(np.float32) * np.float32(2.0 * np.pi / N)
    return (np.cos(angle) + np.sin(angle)).astype(ml_dtypes.bfloat16)


def split(x):
    high = x.astype(bf16)
    return high, (x - high.astype(f32)).astype(bf16)


def outer(left, right, rows):
    return lax.dot_general(
        left[:, rows], right, (((0,), (0,)), ((), ())), preferred_element_type=f32
    )


def main_kernel(
    table_in, holo_in, phase_in, proj_in, mult_in, vol_in, lines_ref, ctf_ref, length_ref,
    newp_out, update_out, ret_out,
    table, holo, work_a, work_b, phase, own_phase, proj, mult, vol,
    terms, relay, arrive, grad, left_h, right_h, left_p, right_p,
    hits, hits_t, sums, image, target, newp, update, picked, band_in, again,
    load_sem, z_send, z_recv, f_send, f_recv, b_send, b_recv, out_sem,
):
    me = lax.axis_index("ang")
    z = lax.axis_index("grp")
    up = lax.rem(z + 1, GROUPS)
    dn = lax.rem(z + GROUPS - 1, GROUPS)
    opp = lax.rem(z + 2, GROUPS)

    def peer(j):
        y = lax.rem(me // 8 + j // 8, 4)
        x = lax.rem(lax.rem(me // 2, 4) + lax.rem(j // 2, 4), 4)
        return y * 8 + x * 2 + lax.rem(me + j, 2)

    def source(j):
        y = lax.rem(me // 8 + 4 - j // 8, 4)
        x = lax.rem(lax.rem(me // 2, 4) + 4 - lax.rem(j // 2, 4), 4)
        return y * 8 + x * 2 + lax.rem(me + j, 2)

    loads = [
        pltpu.make_async_copy(table_in, table, load_sem.at[0]),
        pltpu.make_async_copy(holo_in.at[0, 0], holo, load_sem.at[1]),
        pltpu.make_async_copy(phase_in.at[0], phase, load_sem.at[2]),
        pltpu.make_async_copy(vol_in, vol, load_sem.at[3]),
        pltpu.make_async_copy(
            phase_in.at[0, :, pl.ds(pl.multiple_of(z * QUARTER, QUARTER), QUARTER)],
            own_phase, load_sem.at[4],
        ),
        pltpu.make_async_copy(proj_in.at[0], proj, load_sem.at[5]),
        pltpu.make_async_copy(mult_in.at[0], mult, load_sem.at[6]),
    ]
    for load in loads:
        load.start()

    barrier = pltpu.get_barrier_semaphore()

    def greet(j, _):
        pl.semaphore_signal(barrier, inc=1, device_id=(peer(j), z), device_id_type=MESH)
        return 0

    lax.fori_loop(1, SLABS, greet, 0)
    pl.semaphore_signal(barrier, inc=1, device_id=(me, up), device_id_type=MESH)
    pl.semaphore_signal(barrier, inc=1, device_id=(me, dn), device_id_type=MESH)

    place = lax.broadcasted_iota(jnp.int32, (8, N), 1)
    row = lax.broadcasted_iota(jnp.int32, (8, N), 0)
    folded = jnp.minimum(place, N - place).astype(f32) / N
    freq = folded * folded
    own_coef = ctf_ref[z]
    coef = jnp.where(row == 4, own_coef, 0.0)
    for dist in range(GROUPS):
        coef = jnp.where(row == dist, 2.0 * ctf_ref[dist], coef)
    theta = coef * freq
    sine, cosine = jnp.sin(theta), jnp.cos(theta)
    scale = 2.0 / (N * N)
    zeros8 = jnp.zeros((8, N), f32)

    def pack(parts, height):
        rows = jnp.concatenate(parts, axis=0)
        fill = height - rows.shape[0]
        return jnp.concatenate([rows, jnp.zeros((fill, N), f32)], axis=0).astype(bf16)

    def high(x):
        return x.astype(bf16).astype(f32)

    a_h = jnp.concatenate([sine[4:5], cosine[4:5]], axis=0)
    b_h = jnp.concatenate([cosine[4:5], sine[4:5]], axis=0) * (-scale)
    a_hi, b_hi = high(a_h), high(b_h)
    left_h[...] = pack([a_hi, a_hi, a_h - a_hi], 32)
    right_h[...] = pack([b_hi, b_h - b_hi, b_hi], 32)
    a_p = jnp.concatenate([cosine[0:4], sine[0:4]], axis=0)
    b_p = jnp.concatenate([-cosine[0:4], sine[0:4]], axis=0) * scale
    a_ph, b_ph = high(a_p), high(b_p)
    one = jnp.ones((1, N), f32)
    left_p[...] = pack([a_ph, a_ph, a_p - a_ph, one], 32)
    right_p[...] = pack([b_ph, b_p - b_ph, b_ph, one * (GROUPS * scale)], 32)

    wide = 512

    def columns(i):
        return pl.ds(pl.multiple_of(i * wide, wide), wide)

    def by_table(src, dst):
        def body(i, _):
            cols = columns(i)
            dst[:, cols] = jnp.dot(src[...], table[:, cols], preferred_element_type=f32).astype(bf16)
            return 0

        lax.fori_loop(0, N // wide, body, 0)

    def filtered(src, dst, left, right):
        def body(i, _):
            cols = columns(i)
            spectrum = jnp.dot(table[...], src[:, cols], preferred_element_type=f32)
            weight = lax.dot_general(
                left[...], right[:, cols], (((0,), (0,)), ((), ())), preferred_element_type=f32
            )
            dst[:, cols] = (weight * spectrum).astype(bf16)
            return 0

        lax.fori_loop(0, N // wide, body, 0)

    def of_table(src, dst):
        def body(i, _):
            cols = columns(i)
            dst[:, cols] = jnp.dot(table[...], src[:, cols], preferred_element_type=f32).astype(bf16)
            return 0

        lax.fori_loop(0, N // wide, body, 0)

    loads[0].wait()
    loads[1].wait()
    by_table(holo, work_a)
    filtered(work_a, work_b, left_h, right_h)
    of_table(work_b, work_a)

    def pair_terms(c, first, second, role):
        def cols(q):
            return pl.ds(pl.multiple_of(q * QUARTER + c * CHUNK, CHUNK), CHUNK)

        both = jnp.concatenate([table[:, cols(first)], table[:, cols(second)]], axis=1)
        out = jnp.dot(work_a[...], both, preferred_element_type=f32)
        terms[c, role[0]] = out[:, :CHUNK]
        terms[c, role[1]] = out[:, CHUNK:]

    top, bottom = pl.ds(0, HALF), pl.ds(HALF, HALF)

    def z_copy(c, way, piece):
        target_z = (up, dn)[way]
        if piece == 0:
            src, dst = terms.at[c, OPP, (top, bottom)[way]], relay.at[c, way]
        elif piece == 1:
            rows = (bottom, top)[way]
            src, dst = terms.at[c, (UP, DN)[way], rows], arrive.at[c, way, rows]
        else:
            rows = (top, bottom)[way]
            src, dst = terms.at[c, (UP, DN)[way], rows], arrive.at[c, way, rows]
        return pltpu.make_async_remote_copy(
            src_ref=src, dst_ref=dst,
            send_sem=z_send.at[c, way, piece], recv_sem=z_recv.at[c, way, piece],
            device_id=(me, target_z), device_id_type=MESH,
        )

    def start_piece(c, piece):
        z_copy(c, 0, piece).start()
        z_copy(c, 1, piece).start()

    def pass_on(c):
        z_copy(c, 0, 0).wait_recv()
        terms[c, UP, 0:HALF] += relay[c, 0]
        z_copy(c, 0, 2).start()
        z_copy(c, 1, 0).wait_recv()
        terms[c, DN, HALF:N] += relay[c, 1]
        z_copy(c, 1, 2).start()

    pair_terms(0, opp, z, (OPP, OWN))
    pl.semaphore_wait(barrier, SLABS + 1)
    start_piece(0, 0)
    pair_terms(0, up, dn, (UP, DN))
    start_piece(0, 1)
    pair_terms(1, opp, z, (OPP, OWN))
    pair_terms(1, up, dn, (UP, DN))

    own_length = length_ref[me]

    def build(g, _):
        parts = []
        for k in range(4):
            line = lines_ref[pl.ds(g * 4 + k, 1), :]
            offset = lax.broadcasted_iota(jnp.int32, (BAND, LINES), 0)
            parts.append(jnp.where((line == offset) & (offset < own_length), 1.0, 0.0))
        tile = jnp.concatenate(parts, axis=0)
        at = pl.ds(pl.multiple_of(g * 256, 256), 256)
        hits[at, :] = tile.astype(bf16)
        hits_t[:, at] = jnp.transpose(tile).astype(bf16)
        return 0

    lax.fori_loop(0, 8, build, 0)

    pass_on(0)

    loads[2].wait()
    holo[...] = phase[...].astype(bf16)
    by_table(holo, work_a)
    start_piece(1, 0)
    start_piece(1, 1)
    filtered(work_a, work_b, left_p, right_p)
    pass_on(1)
    own_cols = pl.ds(pl.multiple_of(z * QUARTER, QUARTER), QUARTER)
    part = jnp.dot(work_b[...], table[:, own_cols], preferred_element_type=f32).astype(bf16)
    grad[...] = jnp.dot(table[...], part, preferred_element_type=f32)

    loads[3].wait()
    for v in range(4):
        sums[pl.ds(v * 64, 64), :] = jnp.sum(vol[v].reshape(64, YBLOCK, QUARTER), axis=1)
    sums_hi, sums_lo = split(sums[...])
    sums_split = jnp.concatenate([sums_hi, sums_lo], axis=1)

    def project(g, _):
        at = pl.ds(pl.multiple_of(g * 256, 256), 256)
        both = jnp.dot(hits[at, :], sums_split, preferred_element_type=f32)
        image[at, :] = both[:, :QUARTER] + both[:, QUARTER:]
        return 0

    lax.fori_loop(0, 8, project, 0)
    loads[4].wait()
    loads[5].wait()
    loads[6].wait()

    def f_copy(c, j, slot):
        return pltpu.make_async_remote_copy(
            src_ref=picked.at[c, peer(j)], dst_ref=band_in.at[c, slot],
            send_sem=f_send.at[c, j], recv_sem=f_recv.at[c, slot],
            device_id=(peer(j), z), device_id_type=MESH,
        )

    def b_copy(c, j, slot):
        return pltpu.make_async_remote_copy(
            src_ref=again.at[c, peer(j)], dst_ref=ret_out.at[c, slot],
            send_sem=b_send.at[c, j], recv_sem=b_recv.at[c, slot],
            device_id=(peer(j), z), device_id_type=MESH,
        )

    def new_phases(c):
        cols = pl.ds(c * CHUNK, CHUNK)
        for way in range(2):
            z_copy(c, way, 1).wait_recv()
            z_copy(c, way, 2).wait_recv()
        gradient = grad[:, cols] + terms[c, OWN] + arrive[c, 0] + arrive[c, 1]
        own = own_phase[:, cols]
        dual = mult[:, cols]
        fresh = own - step_phase * (gradient + penalty * (own - proj[:, cols]) + dual)
        newp[:, cols] = fresh
        target[0:N, :] = fresh + dual / penalty

        def pick(s, start):
            picked[c, s] = target[pl.ds(start, BAND), :]
            return start + length_ref[s]

        lax.fori_loop(0, SLABS, pick, jnp.int32(0))

        def send(j, _):
            f_copy(c, j, me).start()
            return 0

        lax.fori_loop(1, SLABS, send, 0)
        band_in[c, me] = picked[c, me]

    def slab(c):
        cols = pl.ds(c * CHUNK, CHUNK)

        def arrived(j, _):
            f_copy(c, j, source(j)).wait_recv()
            return 0

        lax.fori_loop(1, SLABS, arrived, 0)

        def gather(g, total):
            at = pl.ds(pl.multiple_of(g * 256, 256), 256)
            rows = band_in[c, pl.ds(g * 4, 4)].reshape(256, CHUNK)
            hi, lo = split(image[at, cols] - rows)
            both = jnp.concatenate([hi, lo], axis=1)
            return total + jnp.dot(hits_t[:, at], both, preferred_element_type=f32)

        total = lax.fori_loop(0, 8, gather, jnp.zeros((LINES, 2 * CHUNK), f32))
        back = total[:, :CHUNK] + total[:, CHUNK:]
        update[:, cols] = back
        fresh = sums[:, cols] - (step_volume * YBLOCK) * back
        hi, lo = split(fresh)
        both = jnp.concatenate([hi, lo], axis=1)

        def again_rows(g, _):
            at = pl.ds(pl.multiple_of(g * 256, 256), 256)
            out = jnp.dot(hits[at, :], both, preferred_element_type=f32)
            again[c, pl.ds(g * 4, 4)] = (out[:, :CHUNK] + out[:, CHUNK:]).reshape(4, BAND, CHUNK)
            return 0

        lax.fori_loop(0, 8, again_rows, 0)

        def send(j, _):
            b_copy(c, j, me).start()
            return 0

        lax.fori_loop(1, SLABS, send, 0)
        keep = pltpu.make_async_copy(again.at[c, me], ret_out.at[c, me], out_sem.at[c])
        keep.start()
        return keep

    target[N:PAD, :] = jnp.zeros((BAND, CHUNK), f32)
    new_phases(0)
    keep0 = slab(0)
    new_phases(1)
    save_phases = pltpu.make_async_copy(newp, newp_out, out_sem.at[2])
    save_phases.start()
    keep1 = slab(1)
    save_update = pltpu.make_async_copy(update, update_out, out_sem.at[3])
    save_update.start()

    for c in range(CHUNKS):
        for way in range(2):
            for piece in range(3):
                z_copy(c, way, piece).wait_send()

    def finish(j, _):
        for c in range(CHUNKS):
            f_copy(c, j, me).wait_send()
            b_copy(c, j, me).wait_send()
            b_copy(c, j, source(j)).wait_recv()
        return 0

    lax.fori_loop(1, SLABS, finish, 0)
    for copy in (keep0, keep1, save_phases, save_update):
        copy.wait()


def last_kernel(length_ref, ret, newp, mult, vol, update, newp_out, vol_out, mult_out, model):
    i = pl.program_id(0)

    @pl.when(i == 0)
    def _():
        def place(s, start):
            for c in range(CHUNKS):
                model[c, pl.ds(start, BAND), :] = ret[c, s]
            return start + length_ref[s]

        lax.fori_loop(0, SLABS, place, jnp.int32(0))

    fresh = newp[...]
    newp_out[...] = fresh[None]
    rows = pl.ds(pl.multiple_of(i * QUARTER, QUARTER), QUARTER)
    for c in range(CHUNKS):
        cols = slice(c * CHUNK, (c + 1) * CHUNK)
        mult_out[0, :, cols] = mult[0, :, cols] + penalty * (fresh[:, cols] - model[c, rows, :])
    step = step_volume * update[...]
    shaped = jnp.broadcast_to(step[:, None, :], (64, YBLOCK, QUARTER)).reshape(1, N, QUARTER)
    vol_out[...] = vol[...] - shaped


def local(phases, holograms, ctf_phase, projected, multiplier, volume, band_length, line_rows):
    any_spec = pl.BlockSpec(memory_space=pl.ANY)
    smem = pl.BlockSpec(memory_space=pltpu.SMEM)
    vmem = pl.BlockSpec(memory_space=pltpu.VMEM)
    V = pltpu.VMEM
    dma = pltpu.SemaphoreType.DMA
    lines = line_rows.reshape(SLABS, LINES)
    table = jnp.asarray(cas_table())
    newp, update, ret = pl.pallas_call(
        main_kernel,
        out_shape=(
            jax.ShapeDtypeStruct((N, QUARTER), f32),
            jax.ShapeDtypeStruct((LINES, QUARTER), f32),
            jax.ShapeDtypeStruct((CHUNKS, SLABS, BAND, CHUNK), f32),
        ),
        in_specs=[any_spec] * 6 + [vmem, smem, smem],
        out_specs=(any_spec, any_spec, any_spec),
        scratch_shapes=[
            V((N, N), bf16), V((N, N), bf16), V((N, N), bf16), V((N, N), bf16),
            V((N, N), f32), V((N, QUARTER), f32), V((N, QUARTER), f32), V((N, QUARTER), f32),
            V((4, N, QUARTER), f32),
            V((CHUNKS, 4, N, CHUNK), f32), V((CHUNKS, 2, HALF, CHUNK), f32),
            V((CHUNKS, 2, N, CHUNK), f32), V((N, QUARTER), f32),
            V((32, N), bf16), V((32, N), bf16), V((32, N), bf16), V((32, N), bf16),
            V((SLABS * BAND, LINES), bf16), V((LINES, SLABS * BAND), bf16),
            V((LINES, QUARTER), f32), V((SLABS * BAND, QUARTER), f32),
            V((PAD, CHUNK), f32), V((N, QUARTER), f32), V((LINES, QUARTER), f32),
            V((CHUNKS, SLABS, BAND, CHUNK), f32), V((CHUNKS, SLABS, BAND, CHUNK), f32),
            V((CHUNKS, SLABS, BAND, CHUNK), f32),
            dma((7,)), dma((CHUNKS, 2, 3)), dma((CHUNKS, 2, 3)),
            dma((CHUNKS, SLABS)), dma((CHUNKS, SLABS)), dma((CHUNKS, SLABS)), dma((CHUNKS, SLABS)),
            dma((4,)),
        ],
        compiler_params=pltpu.CompilerParams(
            collective_id=0, has_side_effects=True, vmem_limit_bytes=56 * 2**20
        ),
        name="iterate",
    )(table, holograms, phases, projected, multiplier, volume, lines, ctf_phase, band_length)

    whole = lambda *shape: pl.BlockSpec(shape, lambda i: (0,) * len(shape))
    return pl.pallas_call(
        last_kernel,
        grid=(4,),
        out_shape=(
            jax.ShapeDtypeStruct((1, N, QUARTER), f32),
            jax.ShapeDtypeStruct((4, N, QUARTER), f32),
            jax.ShapeDtypeStruct((1, N, QUARTER), f32),
        ),
        in_specs=[
            smem,
            whole(CHUNKS, SLABS, BAND, CHUNK),
            pl.BlockSpec((QUARTER, QUARTER), lambda i: (i, 0)),
            pl.BlockSpec((1, QUARTER, QUARTER), lambda i: (0, i, 0)),
            pl.BlockSpec((1, N, QUARTER), lambda i: (i, 0, 0)),
            pl.BlockSpec((64, QUARTER), lambda i: (i, 0)),
        ],
        out_specs=(
            pl.BlockSpec((1, QUARTER, QUARTER), lambda i: (0, i, 0)),
            pl.BlockSpec((1, N, QUARTER), lambda i: (i, 0, 0)),
            pl.BlockSpec((1, QUARTER, QUARTER), lambda i: (0, i, 0)),
        ),
        scratch_shapes=[V((CHUNKS, PAD, CHUNK), f32)],
        compiler_params=pltpu.CompilerParams(vmem_limit_bytes=40 * 2**20),
        name="finish",
    )(band_length, ret, newp, multiplier, volume, update)


def solution(mesh):
    in_specs = (
        P("ang", None, None),
        P("grp", "ang", None, None),
        P(),
        P("ang", None, "grp"),
        P("ang", None, "grp"),
        P("ang", None, "grp"),
        P(),
        P(None, "ang", None),
    )
    out_specs = (P("ang", None, "grp"), P("ang", None, "grp"), P("ang", None, "grp"))
    return jax.shard_map(local, mesh=mesh, in_specs=in_specs, out_specs=out_specs, check_vma=False)
```

```python
import functools

import jax
import jax.numpy as jnp
import ml_dtypes
import numpy as np
from jax import lax
from jax.experimental import pallas as pl
from jax.experimental.pallas import tpu as pltpu
from jax.sharding import PartitionSpec as P

f32 = jnp.float32
bf16 = jnp.bfloat16
MESH = pl.DeviceIdType.MESH

N = 1024
QUARTER = 256
CHUNK = 128
CHUNKS = 2
SLABS = 32
BAND = 64
LINES = 256
GROUPS = 4
HALF = N // 2
PAD = N + BAND
OPP, OWN, UP, DN = range(4)

step_phase = 0.2
penalty = 0.5
step_volume = 0.004
YBLOCK = 16


def cas_table():
    places = np.arange(N)
    angle = (places[:, None] * places[None, :] % N).astype(np.float32) * np.float32(2.0 * np.pi / N)
    return (np.cos(angle) + np.sin(angle)).astype(ml_dtypes.bfloat16)


def split(x):
    high = x.astype(bf16)
    return high, (x - high.astype(f32)).astype(bf16)


def slab_slot(s):
    y, x, core = s // 8, lax.rem(s // 2, 4), lax.rem(s, 2)
    way = lax.rem(x + y, 2)
    return way, (1 - way) * y + way * x, core, (1 - way) * (x // 2) + way * (y // 2)


def static_slot(s):
    y, x, core = s // 8, s // 2 % 4, s % 2
    return (0, y, core, x // 2) if (x + y) % 2 == 0 else (1, x, core, y // 2)


def main_kernel(
    table_in, holo_in, phase_in, proj_in, mult_in, vol_in, lines_ref, ctf_ref, length_ref,
    newp_out, update_out, ret_out,
    table, holo, work_a, work_b, phase, own_phase, proj, mult, vol,
    terms, relay, arrive, grad, left_h, right_h, left_p, right_p,
    lines, lines_in, hits, hits_t, sums, first_back, target, newp, update,
    picked, inter, part_out, part_in, fresh_sums, again,
    load_sem, z_send, z_recv, l_send, l_recv, a_send, a_recv, b_send, b_recv,
    c_send, c_recv, d_send, d_recv, out_sem, own_sem,
):
    me = lax.axis_index("ang")
    z = lax.axis_index("grp")
    up = lax.rem(z + 1, GROUPS)
    dn = lax.rem(z + GROUPS - 1, GROUPS)
    opp = lax.rem(z + 2, GROUPS)

    y, x, core = me // 8, lax.rem(me // 2, 4), lax.rem(me, 2)
    yh, yl, xh, xl = y // 2, lax.rem(y, 2), x // 2, lax.rem(x, 2)
    kind = lax.rem(x + y, 2)
    own_high = (1 - kind) * xh + kind * yh
    own_pos = (1 - kind) * x + kind * y

    def at_place(py, px, pc):
        return py * 8 + px * 2 + pc

    loads = [
        pltpu.make_async_copy(table_in, table, load_sem.at[0]),
        pltpu.make_async_copy(holo_in.at[0, 0], holo, load_sem.at[1]),
        pltpu.make_async_copy(phase_in.at[0], phase, load_sem.at[2]),
        pltpu.make_async_copy(vol_in, vol, load_sem.at[3]),
        pltpu.make_async_copy(
            phase_in.at[0, :, pl.ds(pl.multiple_of(z * QUARTER, QUARTER), QUARTER)],
            own_phase, load_sem.at[4],
        ),
        pltpu.make_async_copy(proj_in.at[0], proj, load_sem.at[5]),
        pltpu.make_async_copy(mult_in.at[0], mult, load_sem.at[6]),
    ]
    loads[0].start()
    loads[1].start()

    barrier = pltpu.get_barrier_semaphore()

    def greet(device):
        pl.semaphore_signal(barrier, inc=1, device_id=(device, z), device_id_type=MESH)

    for d in range(4):
        for c in range(2):
            if d or c:
                greet(at_place(y, lax.rem(x + d, 4), lax.rem(core + c, 2)))
            if d:
                greet(at_place(lax.rem(y + d, 4), x, lax.rem(core + c, 2)))
    pl.semaphore_signal(barrier, inc=1, device_id=(me, up), device_id_type=MESH)
    pl.semaphore_signal(barrier, inc=1, device_id=(me, dn), device_id_type=MESH)

    place = lax.broadcasted_iota(jnp.int32, (8, N), 1)
    row = lax.broadcasted_iota(jnp.int32, (8, N), 0)
    folded = jnp.minimum(place, N - place).astype(f32) / N
    freq = folded * folded
    own_coef = ctf_ref[z]
    coef = jnp.where(row == 4, own_coef, 0.0)
    for dist in range(GROUPS):
        coef = jnp.where(row == dist, 2.0 * ctf_ref[dist], coef)
    theta = coef * freq
    sine, cosine = jnp.sin(theta), jnp.cos(theta)
    scale = 2.0 / (N * N)
    zeros8 = jnp.zeros((8, N), f32)

    def pack(parts, height):
        rows = jnp.concatenate(parts, axis=0)
        fill = height - rows.shape[0]
        return jnp.concatenate([rows, jnp.zeros((fill, N), f32)], axis=0).astype(bf16)

    def high(x):
        return x.astype(bf16).astype(f32)

    a_h = jnp.concatenate([sine[4:5], cosine[4:5]], axis=0)
    b_h = jnp.concatenate([cosine[4:5], sine[4:5]], axis=0) * (-scale)
    a_hi, b_hi = high(a_h), high(b_h)
    left_h[...] = pack([a_hi, a_hi, a_h - a_hi], 32)
    right_h[...] = pack([b_hi, b_h - b_hi, b_hi], 32)
    a_p = jnp.concatenate([cosine[0:4], sine[0:4]], axis=0)
    b_p = jnp.concatenate([-cosine[0:4], sine[0:4]], axis=0) * scale
    a_ph, b_ph = high(a_p), high(b_p)
    one = jnp.ones((1, N), f32)
    left_p[...] = pack([a_ph, a_ph, a_p - a_ph, one], 32)
    right_p[...] = pack([b_ph, b_p - b_ph, b_ph, one * (GROUPS * scale)], 32)

    wide = 512

    def columns(i):
        return pl.ds(pl.multiple_of(i * wide, wide), wide)

    def by_table(src, dst):
        def body(i, _):
            cols = columns(i)
            dst[:, cols] = jnp.dot(src[...], table[:, cols], preferred_element_type=f32).astype(bf16)
            return 0

        lax.fori_loop(0, N // wide, body, 0)

    def filtered(src, dst, left, right):
        def body(i, _):
            cols = columns(i)
            spectrum = jnp.dot(table[...], src[:, cols], preferred_element_type=f32)
            weight = lax.dot_general(
                left[...], right[:, cols], (((0,), (0,)), ((), ())), preferred_element_type=f32
            )
            dst[:, cols] = (weight * spectrum).astype(bf16)
            return 0

        lax.fori_loop(0, N // wide, body, 0)

    def of_table(src, dst):
        def body(i, _):
            cols = columns(i)
            dst[:, cols] = jnp.dot(table[...], src[:, cols], preferred_element_type=f32).astype(bf16)
            return 0

        lax.fori_loop(0, N // wide, body, 0)

    loads[0].wait()
    loads[1].wait()
    for load in loads[2:]:
        load.start()
    by_table(holo, work_a)
    filtered(work_a, work_b, left_h, right_h)
    of_table(work_b, work_a)

    def pair_terms(c, first, second, role):
        def cols(q):
            return pl.ds(pl.multiple_of(q * QUARTER + c * CHUNK, CHUNK), CHUNK)

        both = jnp.concatenate([table[:, cols(first)], table[:, cols(second)]], axis=1)
        out = jnp.dot(work_a[...], both, preferred_element_type=f32)
        terms[c, role[0]] = out[:, :CHUNK]
        terms[c, role[1]] = out[:, CHUNK:]

    top, bottom = pl.ds(0, HALF), pl.ds(HALF, HALF)

    def z_copy(c, way, piece):
        target_z = (up, dn)[way]
        if piece == 0:
            src, dst = terms.at[c, OPP, (top, bottom)[way]], relay.at[c, way]
        elif piece == 1:
            rows = (bottom, top)[way]
            src, dst = terms.at[c, (UP, DN)[way], rows], arrive.at[c, way, rows]
        else:
            rows = (top, bottom)[way]
            src, dst = terms.at[c, (UP, DN)[way], rows], arrive.at[c, way, rows]
        return pltpu.make_async_remote_copy(
            src_ref=src, dst_ref=dst,
            send_sem=z_send.at[c, way, piece], recv_sem=z_recv.at[c, way, piece],
            device_id=(me, target_z), device_id_type=MESH,
        )

    def start_piece(c, piece):
        z_copy(c, 0, piece).start()
        z_copy(c, 1, piece).start()

    def pass_on(c):
        z_copy(c, 0, 0).wait_recv()
        terms[c, UP, 0:HALF] += relay[c, 0]
        z_copy(c, 0, 2).start()
        z_copy(c, 1, 0).wait_recv()
        terms[c, DN, HALF:N] += relay[c, 1]
        z_copy(c, 1, 2).start()

    def tile(length, line_of):
        parts = []
        for k in range(4):
            offset = lax.broadcasted_iota(jnp.int32, (BAND, LINES), 0)
            parts.append(jnp.where((line_of(k) == offset) & (offset < length), 1.0, 0.0))
        return jnp.concatenate(parts, axis=0)

    def remote(src, dst, send, recv, device):
        return pltpu.make_async_remote_copy(
            src_ref=src, dst_ref=dst, send_sem=send, recv_sem=recv,
            device_id=(device, z), device_id_type=MESH,
        )

    def lane(way, d):
        if way == 0:
            p = lax.rem(y + d, 4)
            return p, at_place(p, x, core)
        p = lax.rem(x + d, 4)
        return p, at_place(y, p, core)

    def rows_for(ref, c, way, p):
        if way == 0:
            return ref.at[c, p // 2, lax.rem(p, 2), :, lax.rem(p, 2)]
        return ref.at[c, :, 1 - lax.rem(p, 2), p // 2, lax.rem(p, 2)]

    mine = (y, x)

    def step(way, d, dc):
        p, _ = lane(way, d)
        pc = lax.rem(core + dc, 2)
        device = at_place(p, x, pc) if way == 0 else at_place(y, p, pc)
        return p, pc, device

    others = [(d, dc) for d in (2, 1, 3) for dc in range(2)] + [(0, 1)]

    def rows_out(c, way, d, dc):
        p, pc, device = step(way, d, dc)
        slot = mine[way] * 2 + core
        return remote(
            picked.at[c, way, p, pc], inter.at[c, way, slot],
            a_send.at[c, way, p * 2 + pc], a_recv.at[c, way, slot], device,
        )

    def rows_in(c, way, d, dc):
        p, pc, device = step(way, d, dc)
        slot = p * 2 + pc
        return remote(
            picked.at[c, way, p, pc], inter.at[c, way, slot],
            a_send.at[c, way, slot], a_recv.at[c, way, slot], device,
        )

    def rows_own(c, way):
        return pltpu.make_async_copy(
            picked.at[c, way, mine[way], core],
            inter.at[c, way, mine[way] * 2 + core], own_sem.at[c, way],
        )

    def owner(way, h):
        return at_place(y, h * 2 + yl, core) if way == 0 else at_place(h * 2 + 1 - xl, x, core)

    def high_of(way, dh):
        return lax.rem((xh, yh)[way] + dh, 2)

    def part_copy(c, way, dh):
        h = high_of(way, dh)
        pos = (x, y)[way]
        return remote(
            part_out.at[c, way, h], part_in.at[c, pos],
            b_send.at[c, way, h], b_recv.at[c, pos], owner(way, h),
        )

    def helper(j):
        pos = lax.rem(own_pos + j, 4)
        return pos, (1 - kind) * at_place(y, pos, core) + kind * at_place(pos, x, core)

    def part_arrival(c, j):
        pos, device = helper(j)
        return remote(part_out.at[c, 0, 0], part_in.at[c, pos], b_send.at[c, 0, 0], b_recv.at[c, pos], device)

    def sums_out(c, j):
        pos, device = helper(j)
        place = (c, kind, own_high)
        return remote(
            fresh_sums.at[place], fresh_sums.at[place], c_send.at[c, j], c_recv.at[place], device
        )

    def sums_in(c, way, dh):
        h = high_of(way, dh)
        place = (c, way, h)
        return remote(
            fresh_sums.at[place], fresh_sums.at[place], c_send.at[c, 1], c_recv.at[place], owner(way, h)
        )

    def back_out(c, way, d, dc):
        p, pc, device = step(way, d, dc)
        slot = p * 2 + pc
        return remote(
            again.at[c, way, slot], ret_out.at[c, way, mine[way], core],
            d_send.at[c, way, slot], d_recv.at[c, way, mine[way] * 2 + core], device,
        )

    def back_in(c, way, d, dc):
        p, pc, device = step(way, d, dc)
        slot = p * 2 + pc
        return remote(
            again.at[c, way, slot], ret_out.at[c, way, p, pc],
            d_send.at[c, way, slot], d_recv.at[c, way, slot], device,
        )

    def back_own(c, way):
        return pltpu.make_async_copy(
            again.at[c, way, mine[way] * 2 + core],
            ret_out.at[c, way, mine[way], core], own_sem.at[c, 2 + way],
        )

    def lines_copy(way, j):
        pos = lax.rem((x, y)[way] + j, 4)
        src = lines.at[:, pos] if way == 0 else lines.at[pos]
        device = at_place(y, pos, core) if way == 0 else at_place(pos, x, core)
        h = (xh, yh)[way]
        return remote(src, lines_in.at[way, h], l_send.at[j], l_recv.at[way, h], device)

    def lines_arrival(way, dh):
        h = high_of(way, dh)
        src = lines.at[:, 0] if way == 0 else lines.at[0]
        return remote(src, lines_in.at[way, h], l_send.at[1], l_recv.at[way, h], owner(way, h))

    def send_lines():
        for a in range(SLABS):
            four = lines_ref[a]
            line = jnp.concatenate([four[v : v + 1] for v in range(4)], axis=1)
            lines[a // 8, a // 2 % 4, a % 2] = jnp.broadcast_to(line, (8, LINES))
        for way in range(2):

            @pl.when(kind == way)
            def _():
                for j in range(1, 4):
                    lines_copy(way, j).start()
                if way == 0:
                    lines_in[0, own_high] = lines[:, x]
                else:
                    lines_in[1, own_high] = lines[y]

    def own_counts():
        own_length = length_ref[me]

        def body(g, total):
            def line_of(k):
                a = g * 4 + k
                return lines[a // 8, lax.rem(a // 2, 4), lax.rem(a, 2)][0:1]

            one = tile(own_length, line_of)
            return total + jnp.dot(
                jnp.transpose(one).astype(bf16), one.astype(bf16), preferred_element_type=f32
            )

        total = lax.fori_loop(0, 8, body, jnp.zeros((LINES, LINES), f32))
        hi, lo = split(sums[...])
        both = jnp.dot(total.astype(bf16), jnp.concatenate([hi, lo], axis=1), preferred_element_type=f32)
        first_back[...] = both[:, :QUARTER] + both[:, QUARTER:]

    def build_hits():
        for way in range(2):
            lines_arrival(way, 1).wait_recv()

            @pl.when(kind != way)
            def _():
                lines_arrival(way, 0).wait_recv()

            def body(n, _):
                h, g = n // 2, lax.rem(n, 2)
                length = length_ref[owner(way, h)]

                def line_of(k):
                    return lines_in[way, h, g * 2 + k // 2, k % 2][0:1]

                one = tile(length, line_of)
                at = pl.ds(pl.multiple_of(g * 256, 256), 256)
                hits[way, h, at, :] = one.astype(bf16)
                hits_t[way, h, :, at] = jnp.transpose(one).astype(bf16)
                return 0

            lax.fori_loop(0, 4, body, 0)

    def send_rows(c):
        for d, dc in others:
            for way in range(2):
                rows_out(c, way, d, dc).start()
        for way in range(2):
            rows_own(c, way).start()

    def send_parts(c):
        for way in range(2):
            for d, dc in others:
                rows_in(c, way, d, dc).wait_recv()
            rows_own(c, way).wait()

            for h in range(2):
                rows = inter[c, way, :, pl.ds(h, 1)].reshape(512, CHUNK)
                hi, lo = split(rows)
                both = jnp.dot(
                    hits_t[way, h], jnp.concatenate([hi, lo], axis=1), preferred_element_type=f32
                )
                part_out[c, way, h] = both[:, :CHUNK] + both[:, CHUNK:]
            part_copy(c, way, 1).start()

            @pl.when(kind != way)
            def _():
                part_copy(c, way, 0).start()

    def send_sums(c):
        cols = pl.ds(c * CHUNK, CHUNK)
        for j in range(1, 4):
            part_arrival(c, j).wait_recv()
        total = part_out[c, kind, own_high]
        for j in range(1, 4):
            total = total + part_in[c, lax.rem(own_pos + j, 4)]
        back = first_back[:, cols] - total
        update[:, cols] = back
        fresh_sums[c, kind, own_high] = sums[:, cols] - (step_volume * YBLOCK) * back
        for j in range(1, 4):
            sums_out(c, j).start()

    def send_back(c):
        for way in range(2):
            sums_in(c, way, 1).wait_recv()

            @pl.when(kind != way)
            def _():
                sums_in(c, way, 0).wait_recv()

            for h in range(2):
                hi, lo = split(fresh_sums[c, way, h])
                both = jnp.dot(
                    hits[way, h], jnp.concatenate([hi, lo], axis=1), preferred_element_type=f32
                )
                again[c, way, :, h] = (both[:, :CHUNK] + both[:, CHUNK:]).reshape(8, BAND, CHUNK)
            for d, dc in others:
                back_out(c, way, d, dc).start()
            back_own(c, way).start()

    def wait_all(c):
        for way in range(2):
            for d, dc in others:
                back_in(c, way, d, dc).wait_recv()
                rows_out(c, way, d, dc).wait_send()
                back_out(c, way, d, dc).wait_send()
            back_own(c, way).wait()
            part_copy(c, way, 1).wait_send()

            @pl.when(kind != way)
            def _():
                part_copy(c, way, 0).wait_send()

        for j in range(1, 4):
            sums_out(c, j).wait_send()

    def new_phases(c):
        cols = pl.ds(c * CHUNK, CHUNK)
        for way in range(2):
            z_copy(c, way, 1).wait_recv()
            z_copy(c, way, 2).wait_recv()
        gradient = grad[:, cols] + terms[c, OWN] + arrive[c, 0] + arrive[c, 1]
        own = own_phase[:, cols]
        dual = mult[:, cols]
        fresh = own - step_phase * (gradient + penalty * (own - proj[:, cols]) + dual)
        newp[:, cols] = fresh
        target[0:N, :] = fresh + dual / penalty

        start = 0
        for s in range(SLABS):
            picked[(c, *static_slot(s))] = target[pl.ds(start, BAND), :]
            start = start + length_ref[s]
        send_rows(c)

    pair_terms(0, opp, z, (OPP, OWN))
    pl.semaphore_wait(barrier, 15)
    start_piece(0, 0)
    pair_terms(0, up, dn, (UP, DN))
    pair_terms(1, opp, z, (OPP, OWN))
    send_lines()
    start_piece(0, 1)
    pair_terms(1, up, dn, (UP, DN))

    loads[2].wait()
    holo[...] = phase[...].astype(bf16)
    by_table(holo, work_a)
    pass_on(0)
    filtered(work_a, work_b, left_p, right_p)
    own_cols = pl.ds(pl.multiple_of(z * QUARTER, QUARTER), QUARTER)
    part = jnp.dot(work_b[...], table[:, own_cols], preferred_element_type=f32).astype(bf16)
    start_piece(1, 0)
    grad[...] = jnp.dot(table[...], part, preferred_element_type=f32)

    loads[3].wait()
    for v in range(4):
        sums[pl.ds(v * 64, 64), :] = jnp.sum(vol[v].reshape(64, YBLOCK, QUARTER), axis=1)
    for load in loads[4:]:
        load.wait()
    start_piece(1, 1)
    target[N:PAD, :] = jnp.zeros((BAND, CHUNK), f32)

    new_phases(0)
    own_counts()
    pass_on(1)
    build_hits()
    send_parts(0)
    new_phases(1)
    save_phases = pltpu.make_async_copy(newp, newp_out, out_sem.at[0])
    save_phases.start()
    send_sums(0)
    send_parts(1)
    send_back(0)
    send_sums(1)
    save_update = pltpu.make_async_copy(update, update_out, out_sem.at[1])
    save_update.start()
    send_back(1)

    for way in range(2):

        @pl.when(kind == way)
        def _():
            for j in range(1, 4):
                lines_copy(way, j).wait_send()

    for c in range(CHUNKS):
        for way in range(2):
            for piece in range(3):
                z_copy(c, way, piece).wait_send()
        wait_all(c)
    save_phases.wait()
    save_update.wait()


def last_kernel(length_ref, ret, newp, mult, vol, update, newp_out, vol_out, mult_out, model, at_row):
    i = pl.program_id(0)

    @pl.when(i == 0)
    def _():
        at_row[0] = 0

    @pl.when(i < 4)
    def _():
        def place(s, start):
            for c in range(CHUNKS):
                model[c, pl.ds(start, BAND), :] = ret[(c, *slab_slot(i * 8 + s))]
            return start + length_ref[i * 8 + s]

        at_row[0] = lax.fori_loop(0, 8, place, at_row[0])

    @pl.when(i >= 4)
    def _():
        fresh = newp[...]
        newp_out[...] = fresh[None]
        rows = pl.ds(pl.multiple_of((i - 4) * QUARTER, QUARTER), QUARTER)
        for c in range(CHUNKS):
            cols = slice(c * CHUNK, (c + 1) * CHUNK)
            mult_out[0, :, cols] = mult[0, :, cols] + penalty * (fresh[:, cols] - model[c, rows, :])

    change = step_volume * update[...]
    shaped = jnp.broadcast_to(change[:, None, :], (32, YBLOCK, QUARTER)).reshape(1, HALF, QUARTER)
    vol_out[...] = vol[...] - shaped


def local(phases, holograms, ctf_phase, projected, multiplier, volume, band_length, line_rows):
    any_spec = pl.BlockSpec(memory_space=pl.ANY)
    smem = pl.BlockSpec(memory_space=pltpu.SMEM)
    vmem = pl.BlockSpec(memory_space=pltpu.VMEM)
    V = pltpu.VMEM
    dma = pltpu.SemaphoreType.DMA
    table = jnp.asarray(cas_table())
    newp, update, ret = pl.pallas_call(
        main_kernel,
        out_shape=(
            jax.ShapeDtypeStruct((N, QUARTER), f32),
            jax.ShapeDtypeStruct((LINES, QUARTER), f32),
            jax.ShapeDtypeStruct((CHUNKS, 2, 4, 2, 2, BAND, CHUNK), f32),
        ),
        in_specs=[any_spec] * 6 + [vmem, smem, smem],
        out_specs=(any_spec, any_spec, any_spec),
        scratch_shapes=[
            V((N, N), bf16), V((N, N), bf16), V((N, N), bf16), V((N, N), bf16),
            V((N, N), f32), V((N, QUARTER), f32), V((N, QUARTER), f32), V((N, QUARTER), f32),
            V((4, N, QUARTER), f32),
            V((CHUNKS, 4, N, CHUNK), f32), V((CHUNKS, 2, HALF, CHUNK), f32),
            V((CHUNKS, 2, N, CHUNK), f32), V((N, QUARTER), f32),
            V((32, N), bf16), V((32, N), bf16), V((32, N), bf16), V((32, N), bf16),
            V((4, 4, 2, 8, LINES), jnp.int32), V((2, 2, 4, 2, 8, LINES), jnp.int32),
            V((2, 2, 512, LINES), bf16), V((2, 2, LINES, 512), bf16),
            V((LINES, QUARTER), f32), V((LINES, QUARTER), f32),
            V((PAD, CHUNK), f32), V((N, QUARTER), f32), V((LINES, QUARTER), f32),
            V((CHUNKS, 2, 4, 2, 2, BAND, CHUNK), f32), V((CHUNKS, 2, 8, 2, BAND, CHUNK), f32),
            V((CHUNKS, 2, 2, LINES, CHUNK), f32), V((CHUNKS, 4, LINES, CHUNK), f32),
            V((CHUNKS, 2, 2, LINES, CHUNK), f32), V((CHUNKS, 2, 8, 2, BAND, CHUNK), f32),
            dma((7,)), dma((CHUNKS, 2, 3)), dma((CHUNKS, 2, 3)),
            dma((4,)), dma((2, 2)), dma((CHUNKS, 2, 8)), dma((CHUNKS, 2, 8)),
            dma((CHUNKS, 2, 2)), dma((CHUNKS, 4)), dma((CHUNKS, 4)), dma((CHUNKS, 2, 2)),
            dma((CHUNKS, 2, 8)), dma((CHUNKS, 2, 8)), dma((2,)), dma((CHUNKS, 4)),
        ],
        compiler_params=pltpu.CompilerParams(
            collective_id=0, has_side_effects=True, vmem_limit_bytes=56 * 2**20
        ),
        name="iterate",
    )(table, holograms, phases, projected, multiplier, volume, line_rows, ctf_phase, band_length)

    rows_spec = pl.BlockSpec((1, QUARTER, QUARTER), lambda i: (0, jnp.maximum(i - 4, 0), 0))
    vol_spec = pl.BlockSpec((1, HALF, QUARTER), lambda i: (i // 2, lax.rem(i, 2), 0))
    return pl.pallas_call(
        last_kernel,
        grid=(8,),
        out_shape=(
            jax.ShapeDtypeStruct((1, N, QUARTER), f32),
            jax.ShapeDtypeStruct((4, N, QUARTER), f32),
            jax.ShapeDtypeStruct((1, N, QUARTER), f32),
        ),
        in_specs=[
            smem,
            pl.BlockSpec((CHUNKS, 2, 4, 2, 2, BAND, CHUNK), lambda i: (0,) * 7),
            pl.BlockSpec((QUARTER, QUARTER), lambda i: (jnp.maximum(i - 4, 0), 0)),
            rows_spec,
            vol_spec,
            pl.BlockSpec((32, QUARTER), lambda i: (i, 0)),
        ],
        out_specs=(rows_spec, vol_spec, rows_spec),
        scratch_shapes=[V((CHUNKS, PAD, CHUNK), f32), pltpu.SMEM((1,), jnp.int32)],
        compiler_params=pltpu.CompilerParams(vmem_limit_bytes=60 * 2**20),
        name="finish",
    )(band_length, ret, newp, multiplier, volume, update)


def solution(mesh):
    in_specs = (
        P("ang", None, None),
        P("grp", "ang", None, None),
        P(),
        P("ang", None, "grp"),
        P("ang", None, "grp"),
        P("ang", None, "grp"),
        P(),
        P(None, "ang", None),
    )
    out_specs = (P("ang", None, "grp"), P("ang", None, "grp"), P("ang", None, "grp"))
    return jax.shard_map(local, mesh=mesh, in_specs=in_specs, out_specs=out_specs, check_vma=False)
```

```python
import functools

import jax
import jax.numpy as jnp
import ml_dtypes
import numpy as np
from jax import lax
from jax.experimental import pallas as pl
from jax.experimental.pallas import tpu as pltpu
from jax.sharding import PartitionSpec as P

f32 = jnp.float32
bf16 = jnp.bfloat16
MESH = pl.DeviceIdType.MESH

N = 1024
QUARTER = 256
CHUNK = 128
CHUNKS = 2
SLABS = 32
BAND = 64
LINES = 256
GROUPS = 4
HALF = N // 2
PAD = N + BAND
OPP, OWN, UP, DN = range(4)

step_phase = 0.2
penalty = 0.5
step_volume = 0.004
YBLOCK = 16


def cas_table():
    places = np.arange(N)
    angle = (places[:, None] * places[None, :] % N).astype(np.float32) * np.float32(2.0 * np.pi / N)
    return (np.cos(angle) + np.sin(angle)).astype(ml_dtypes.bfloat16)


def split(x):
    high = x.astype(bf16)
    return high, (x - high.astype(f32)).astype(bf16)


def static_slot(s):
    y, x, core = s // 8, s // 2 % 4, s % 2
    return (0, y, core, x // 2) if (x + y) % 2 == 0 else (1, x, core, y // 2)


def main_kernel(
    table_in, holo_in, phase_in, proj_in, mult_in, vol_in, lines_ref, ctf_ref, length_ref,
    newp_out, update_out, ret_out,
    table, holo, work_a, work_b, phase, own_phase, proj, mult, vol,
    terms, relay, arrive, grad, left_h, right_h, left_p, right_p,
    lines, lines_in, hits, hits_t, sums, first_back, target, newp, update,
    picked, inter, part_out, part_in, fresh_sums, again,
    load_sem, z_send, z_recv, l_send, l_recv, a_send, a_recv, b_send, b_recv,
    c_send, c_recv, d_send, d_recv, out_sem, own_sem,
):
    me = lax.axis_index("ang")
    z = lax.axis_index("grp")
    up = lax.rem(z + 1, GROUPS)
    dn = lax.rem(z + GROUPS - 1, GROUPS)
    opp = lax.rem(z + 2, GROUPS)

    y, x, core = me // 8, lax.rem(me // 2, 4), lax.rem(me, 2)
    yh, yl, xh, xl = y // 2, lax.rem(y, 2), x // 2, lax.rem(x, 2)
    kind = lax.rem(x + y, 2)
    own_high = (1 - kind) * xh + kind * yh
    own_pos = (1 - kind) * x + kind * y

    def at_place(py, px, pc):
        return py * 8 + px * 2 + pc

    loads = [
        pltpu.make_async_copy(table_in, table, load_sem.at[0]),
        pltpu.make_async_copy(holo_in.at[0, 0], holo, load_sem.at[1]),
        pltpu.make_async_copy(phase_in.at[0], phase, load_sem.at[2]),
        pltpu.make_async_copy(vol_in, vol, load_sem.at[3]),
        pltpu.make_async_copy(
            phase_in.at[0, :, pl.ds(pl.multiple_of(z * QUARTER, QUARTER), QUARTER)],
            own_phase, load_sem.at[4],
        ),
        pltpu.make_async_copy(proj_in.at[0], proj, load_sem.at[5]),
        pltpu.make_async_copy(mult_in.at[0], mult, load_sem.at[6]),
    ]
    loads[0].start()
    loads[1].start()

    barrier = pltpu.get_barrier_semaphore()

    def greet(device):
        pl.semaphore_signal(barrier, inc=1, device_id=(device, z), device_id_type=MESH)

    for d in range(4):
        for c in range(2):
            if d or c:
                greet(at_place(y, lax.rem(x + d, 4), lax.rem(core + c, 2)))
            if d:
                greet(at_place(lax.rem(y + d, 4), x, lax.rem(core + c, 2)))
    pl.semaphore_signal(barrier, inc=1, device_id=(me, up), device_id_type=MESH)
    pl.semaphore_signal(barrier, inc=1, device_id=(me, dn), device_id_type=MESH)

    place = lax.broadcasted_iota(jnp.int32, (8, N), 1)
    row = lax.broadcasted_iota(jnp.int32, (8, N), 0)
    folded = jnp.minimum(place, N - place).astype(f32) / N
    freq = folded * folded
    own_coef = ctf_ref[z]
    coef = jnp.where(row == 4, own_coef, 0.0)
    for dist in range(GROUPS):
        coef = jnp.where(row == dist, 2.0 * ctf_ref[dist], coef)
    theta = coef * freq
    sine, cosine = jnp.sin(theta), jnp.cos(theta)
    scale = 2.0 / (N * N)
    zeros8 = jnp.zeros((8, N), f32)

    def pack(parts, height):
        rows = jnp.concatenate(parts, axis=0)
        fill = height - rows.shape[0]
        return jnp.concatenate([rows, jnp.zeros((fill, N), f32)], axis=0).astype(bf16)

    def high(x):
        return x.astype(bf16).astype(f32)

    a_h = jnp.concatenate([sine[4:5], cosine[4:5]], axis=0)
    b_h = jnp.concatenate([cosine[4:5], sine[4:5]], axis=0) * (-scale)
    a_hi, b_hi = high(a_h), high(b_h)
    left_h[...] = pack([a_hi, a_hi, a_h - a_hi], 32)
    right_h[...] = pack([b_hi, b_h - b_hi, b_hi], 32)
    a_p = jnp.concatenate([cosine[0:4], sine[0:4]], axis=0)
    b_p = jnp.concatenate([-cosine[0:4], sine[0:4]], axis=0) * scale
    a_ph, b_ph = high(a_p), high(b_p)
    one = jnp.ones((1, N), f32)
    left_p[...] = pack([a_ph, a_ph, a_p - a_ph, one], 32)
    right_p[...] = pack([b_ph, b_p - b_ph, b_ph, one * (GROUPS * scale)], 32)

    wide = 512

    def columns(i):
        return pl.ds(pl.multiple_of(i * wide, wide), wide)

    def by_table(src, dst):
        def body(i, _):
            cols = columns(i)
            dst[:, cols] = jnp.dot(src[...], table[:, cols], preferred_element_type=f32).astype(bf16)
            return 0

        lax.fori_loop(0, N // wide, body, 0)

    def filtered(src, dst, left, right):
        def body(i, _):
            cols = columns(i)
            spectrum = jnp.dot(table[...], src[:, cols], preferred_element_type=f32)
            weight = lax.dot_general(
                left[...], right[:, cols], (((0,), (0,)), ((), ())), preferred_element_type=f32
            )
            dst[:, cols] = (weight * spectrum).astype(bf16)
            return 0

        lax.fori_loop(0, N // wide, body, 0)

    def of_table(src, dst):
        def body(i, _):
            cols = columns(i)
            dst[:, cols] = jnp.dot(table[...], src[:, cols], preferred_element_type=f32).astype(bf16)
            return 0

        lax.fori_loop(0, N // wide, body, 0)

    loads[0].wait()
    loads[1].wait()
    for load in loads[2:]:
        load.start()
    by_table(holo, work_a)
    filtered(work_a, work_b, left_h, right_h)
    of_table(work_b, work_a)

    def pair_terms(c, first, second, role):
        def cols(q):
            return pl.ds(pl.multiple_of(q * QUARTER + c * CHUNK, CHUNK), CHUNK)

        both = jnp.concatenate([table[:, cols(first)], table[:, cols(second)]], axis=1)
        out = jnp.dot(work_a[...], both, preferred_element_type=f32)
        terms[c, role[0]] = out[:, :CHUNK]
        terms[c, role[1]] = out[:, CHUNK:]

    top, bottom = pl.ds(0, HALF), pl.ds(HALF, HALF)

    def z_copy(c, way, piece):
        target_z = (up, dn)[way]
        if piece == 0:
            src, dst = terms.at[c, OPP, (top, bottom)[way]], relay.at[c, way]
        elif piece == 1:
            rows = (bottom, top)[way]
            src, dst = terms.at[c, (UP, DN)[way], rows], arrive.at[c, way, rows]
        else:
            rows = (top, bottom)[way]
            src, dst = terms.at[c, (UP, DN)[way], rows], arrive.at[c, way, rows]
        return pltpu.make_async_remote_copy(
            src_ref=src, dst_ref=dst,
            send_sem=z_send.at[c, way, piece], recv_sem=z_recv.at[c, way, piece],
            device_id=(me, target_z), device_id_type=MESH,
        )

    def start_piece(c, piece):
        z_copy(c, 0, piece).start()
        z_copy(c, 1, piece).start()

    def pass_on(c):
        z_copy(c, 0, 0).wait_recv()
        terms[c, UP, 0:HALF] += relay[c, 0]
        z_copy(c, 0, 2).start()
        z_copy(c, 1, 0).wait_recv()
        terms[c, DN, HALF:N] += relay[c, 1]
        z_copy(c, 1, 2).start()

    def tile(length, line_of):
        parts = []
        for k in range(4):
            offset = lax.broadcasted_iota(jnp.int32, (BAND, LINES), 0)
            parts.append(jnp.where((line_of(k) == offset) & (offset < length), 1.0, 0.0))
        return jnp.concatenate(parts, axis=0)

    def remote(src, dst, send, recv, device):
        return pltpu.make_async_remote_copy(
            src_ref=src, dst_ref=dst, send_sem=send, recv_sem=recv,
            device_id=(device, z), device_id_type=MESH,
        )

    def lane(way, d):
        if way == 0:
            p = lax.rem(y + d, 4)
            return p, at_place(p, x, core)
        p = lax.rem(x + d, 4)
        return p, at_place(y, p, core)

    def rows_for(ref, c, way, p):
        if way == 0:
            return ref.at[c, p // 2, lax.rem(p, 2), :, lax.rem(p, 2)]
        return ref.at[c, :, 1 - lax.rem(p, 2), p // 2, lax.rem(p, 2)]

    mine = (y, x)

    def step(way, d, dc):
        p, _ = lane(way, d)
        pc = lax.rem(core + dc, 2)
        device = at_place(p, x, pc) if way == 0 else at_place(y, p, pc)
        return p, pc, device

    others = [(d, dc) for d in (2, 1, 3) for dc in range(2)] + [(0, 1)]

    def rows_out(c, h, way, d, dc):
        p, pc, device = step(way, d, dc)
        slot = mine[way] * 2 + core
        return remote(
            picked.at[c, way, p, pc, h], inter.at[c, way, slot, h],
            a_send.at[c, h, way, p * 2 + pc], a_recv.at[c, h, way, slot], device,
        )

    def rows_in(c, h, way, d, dc):
        p, pc, device = step(way, d, dc)
        slot = p * 2 + pc
        return remote(
            picked.at[c, way, p, pc, h], inter.at[c, way, slot, h],
            a_send.at[c, h, way, slot], a_recv.at[c, h, way, slot], device,
        )

    def rows_own(c, h, way):
        return pltpu.make_async_copy(
            picked.at[c, way, mine[way], core, h],
            inter.at[c, way, mine[way] * 2 + core, h], own_sem.at[c, h, way],
        )

    def owner(way, h):
        return at_place(y, h * 2 + yl, core) if way == 0 else at_place(h * 2 + 1 - xl, x, core)

    def elsewhere(way, h):
        return pl.when(kind * 2 + own_high != way * 2 + h)

    def part_copy(c, h, way):
        pos = (x, y)[way]
        return remote(
            part_out.at[c, way, h], part_in.at[c, pos],
            b_send.at[c, way, h], b_recv.at[c, pos], owner(way, h),
        )

    def helper(j):
        pos = lax.rem(own_pos + j, 4)
        return pos, (1 - kind) * at_place(y, pos, core) + kind * at_place(pos, x, core)

    def part_arrival(c, j):
        pos, device = helper(j)
        return remote(part_out.at[c, 0, 0], part_in.at[c, pos], b_send.at[c, 0, 0], b_recv.at[c, pos], device)

    def sums_out(c, j):
        pos, device = helper(j)
        place = (c, kind, own_high)
        return remote(
            fresh_sums.at[place], fresh_sums.at[place], c_send.at[c, j], c_recv.at[place], device
        )

    def sums_in(c, h, way):
        place = (c, way, h)
        return remote(
            fresh_sums.at[place], fresh_sums.at[place], c_send.at[c, 1], c_recv.at[place], owner(way, h)
        )

    def back_out(c, h, way, d, dc):
        p, pc, device = step(way, d, dc)
        slot = p * 2 + pc
        return remote(
            again.at[c, way, slot, h], ret_out.at[c, way, mine[way], core, h],
            d_send.at[c, h, way, slot], d_recv.at[c, h, way, mine[way] * 2 + core], device,
        )

    def back_in(c, h, way, d, dc):
        p, pc, device = step(way, d, dc)
        slot = p * 2 + pc
        return remote(
            again.at[c, way, slot, h], ret_out.at[c, way, p, pc, h],
            d_send.at[c, h, way, slot], d_recv.at[c, h, way, slot], device,
        )

    def back_own(c, h, way):
        return pltpu.make_async_copy(
            again.at[c, way, mine[way] * 2 + core, h],
            ret_out.at[c, way, mine[way], core, h], own_sem.at[c, h, 2 + way],
        )

    def lines_copy(way, j):
        pos = lax.rem((x, y)[way] + j, 4)
        src = lines.at[:, pos] if way == 0 else lines.at[pos]
        device = at_place(y, pos, core) if way == 0 else at_place(pos, x, core)
        h = (xh, yh)[way]
        return remote(src, lines_in.at[way, h], l_send.at[j], l_recv.at[way, h], device)

    def lines_arrival(way, h):
        src = lines.at[:, 0] if way == 0 else lines.at[0]
        return remote(src, lines_in.at[way, h], l_send.at[1], l_recv.at[way, h], owner(way, h))

    def send_lines():
        for a in range(SLABS):
            four = lines_ref[a]
            line = jnp.concatenate([four[v : v + 1] for v in range(4)], axis=1)
            lines[a // 8, a // 2 % 4, a % 2] = jnp.broadcast_to(line, (8, LINES))
        for way in range(2):

            @pl.when(kind == way)
            def _():
                for j in range(1, 4):
                    lines_copy(way, j).start()
                if way == 0:
                    lines_in[0, own_high] = lines[:, x]
                else:
                    lines_in[1, own_high] = lines[y]

    def own_counts():
        own_length = length_ref[me]

        def body(g, total):
            def line_of(k):
                a = g * 4 + k
                return lines[a // 8, lax.rem(a // 2, 4), lax.rem(a, 2)][0:1]

            one = tile(own_length, line_of)
            return total + jnp.dot(
                jnp.transpose(one).astype(bf16), one.astype(bf16), preferred_element_type=f32
            )

        total = lax.fori_loop(0, 8, body, jnp.zeros((LINES, LINES), f32))
        hi, lo = split(sums[...])
        both = jnp.dot(total.astype(bf16), jnp.concatenate([hi, lo], axis=1), preferred_element_type=f32)
        first_back[...] = both[:, :QUARTER] + both[:, QUARTER:]

    def build_hits():
        for way in range(2):
            for h in range(2):

                @elsewhere(way, h)
                def _():
                    lines_arrival(way, h).wait_recv()

            def body(n, _):
                h, g = n // 2, lax.rem(n, 2)
                length = length_ref[owner(way, h)]

                def line_of(k):
                    return lines_in[way, h, g * 2 + k // 2, k % 2][0:1]

                one = tile(length, line_of)
                at = pl.ds(pl.multiple_of(g * 256, 256), 256)
                hits[way, h, at, :] = one.astype(bf16)
                hits_t[way, h, :, at] = jnp.transpose(one).astype(bf16)
                return 0

            lax.fori_loop(0, 4, body, 0)

    def send_rows(c, h):
        for d, dc in others:
            for way in range(2):
                rows_out(c, h, way, d, dc).start()
        for way in range(2):
            rows_own(c, h, way).start()

    def send_parts(c, h):
        for way in range(2):
            for d, dc in others:
                rows_in(c, h, way, d, dc).wait_recv()
            rows_own(c, h, way).wait()
            rows = inter[c, way, :, pl.ds(h, 1)].reshape(512, CHUNK)
            hi, lo = split(rows)
            both = jnp.dot(hits_t[way, h], jnp.concatenate([hi, lo], axis=1), preferred_element_type=f32)
            part_out[c, way, h] = both[:, :CHUNK] + both[:, CHUNK:]

            @elsewhere(way, h)
            def _():
                part_copy(c, h, way).start()

    def send_sums(c):
        cols = pl.ds(c * CHUNK, CHUNK)
        for j in range(1, 4):
            part_arrival(c, j).wait_recv()
        total = part_out[c, kind, own_high]
        for j in range(1, 4):
            total = total + part_in[c, lax.rem(own_pos + j, 4)]
        back = first_back[:, cols] - total
        update[:, cols] = back
        fresh_sums[c, kind, own_high] = sums[:, cols] - (step_volume * YBLOCK) * back
        for j in range(1, 4):
            sums_out(c, j).start()

    def send_back(c, h):
        for way in range(2):

            @elsewhere(way, h)
            def _():
                sums_in(c, h, way).wait_recv()

            hi, lo = split(fresh_sums[c, way, h])
            both = jnp.dot(hits[way, h], jnp.concatenate([hi, lo], axis=1), preferred_element_type=f32)
            again[c, way, :, pl.ds(h, 1)] = (both[:, :CHUNK] + both[:, CHUNK:]).reshape(8, 1, BAND, CHUNK)
            for d, dc in others:
                back_out(c, h, way, d, dc).start()
            back_own(c, h, way).start()

    def wait_all(c):
        for h in range(2):
            for way in range(2):
                for d, dc in others:
                    back_in(c, h, way, d, dc).wait_recv()
                    if h == 1:
                        rows_out(c, h, way, d, dc).wait_send()
                    back_out(c, h, way, d, dc).wait_send()
                back_own(c, h, way).wait()

                @elsewhere(way, h)
                def _():
                    part_copy(c, h, way).wait_send()

        for j in range(1, 4):
            sums_out(c, j).wait_send()

    def new_phases(c):
        cols = pl.ds(c * CHUNK, CHUNK)
        for way in range(2):
            z_copy(c, way, 1).wait_recv()
            z_copy(c, way, 2).wait_recv()
        gradient = grad[:, cols] + terms[c, OWN] + arrive[c, 0] + arrive[c, 1]
        own = own_phase[:, cols]
        dual = mult[:, cols]
        fresh = own - step_phase * (gradient + penalty * (own - proj[:, cols]) + dual)
        newp[:, cols] = fresh
        target[0:N, :] = fresh + dual / penalty

        for h in range(2):
            start = 0
            for s in range(SLABS):
                slot = static_slot(s)
                if slot[3] == h:
                    picked[(c, *slot)] = target[pl.ds(start, BAND), :]
                start = start + length_ref[s]
            send_rows(c, h)
            if h == 0:
                for d, dc in others:
                    for way in range(2):
                        rows_out(c, 0, way, d, dc).wait_send()

    pair_terms(0, opp, z, (OPP, OWN))
    pl.semaphore_wait(barrier, 15)
    start_piece(0, 0)
    pair_terms(0, up, dn, (UP, DN))
    pair_terms(1, opp, z, (OPP, OWN))
    send_lines()
    start_piece(0, 1)
    pair_terms(1, up, dn, (UP, DN))

    loads[2].wait()
    holo[...] = phase[...].astype(bf16)
    by_table(holo, work_a)
    pass_on(0)
    filtered(work_a, work_b, left_p, right_p)
    own_cols = pl.ds(pl.multiple_of(z * QUARTER, QUARTER), QUARTER)
    part = jnp.dot(work_b[...], table[:, own_cols], preferred_element_type=f32).astype(bf16)
    start_piece(1, 0)
    grad[...] = jnp.dot(table[...], part, preferred_element_type=f32)

    loads[3].wait()
    for v in range(4):
        sums[pl.ds(v * 64, 64), :] = jnp.sum(vol[v].reshape(64, YBLOCK, QUARTER), axis=1)
    for load in loads[4:]:
        load.wait()
    start_piece(1, 1)
    target[N:PAD, :] = jnp.zeros((BAND, CHUNK), f32)

    new_phases(0)
    own_counts()
    pass_on(1)
    build_hits()
    send_parts(0,0)
    send_parts(0,1)
    new_phases(1)
    save_phases = pltpu.make_async_copy(newp, newp_out, out_sem.at[0])
    save_phases.start()
    send_sums(0)
    send_parts(1,0)
    send_parts(1,1)
    send_back(0,0)
    send_back(0,1)
    send_sums(1)
    save_update = pltpu.make_async_copy(update, update_out, out_sem.at[1])
    save_update.start()
    send_back(1,0)
    send_back(1,1)

    for way in range(2):

        @pl.when(kind == way)
        def _():
            for j in range(1, 4):
                lines_copy(way, j).wait_send()

    for c in range(CHUNKS):
        for way in range(2):
            for piece in range(3):
                z_copy(c, way, piece).wait_send()
        wait_all(c)
    save_phases.wait()
    save_update.wait()


def last_kernel(
    length_ref, ret_in, newp_in, mult_in, vol_in, update_in, newp_out, vol_out, mult_out,
    ret, newp, mult, vol, update, model, sem_in, sem_out,
):
    load_update = pltpu.make_async_copy(update_in, update, sem_in.at[0])
    load_vol = [pltpu.make_async_copy(vol_in.at[v], vol.at[v], sem_in.at[1 + v]) for v in range(4)]
    load_ret = pltpu.make_async_copy(ret_in, ret, sem_in.at[5])
    load_newp = pltpu.make_async_copy(newp_in, newp, sem_in.at[6])
    load_mult = pltpu.make_async_copy(mult_in.at[0], mult, sem_in.at[7])
    for load in (load_update, load_newp, load_vol[0], load_ret, load_vol[1], load_mult, load_vol[2], load_vol[3]):
        load.start()

    stores = []

    def store(src, dst):
        copy = pltpu.make_async_copy(src, dst, sem_out.at[len(stores)])
        copy.start()
        stores.append(copy)

    def volume_part(v):
        load_vol[v].wait()
        change = step_volume * update[v * 64 : v * 64 + 64, :]
        shaped = jnp.broadcast_to(change[:, None, :], (64, YBLOCK, QUARTER)).reshape(N, QUARTER)
        vol[v] = vol[v] - shaped
        store(vol.at[v], vol_out.at[v])

    load_update.wait()
    load_newp.wait()
    store(newp, newp_out.at[0])
    volume_part(0)
    load_ret.wait()
    start = 0
    for s in range(SLABS):
        for c in range(CHUNKS):
            model[c, pl.ds(start, BAND), :] = ret[(c, *static_slot(s))]
        start = start + length_ref[s]
    volume_part(1)
    load_mult.wait()
    for c in range(CHUNKS):
        cols = slice(c * CHUNK, (c + 1) * CHUNK)
        mult[:, cols] = mult[:, cols] + penalty * (newp[:, cols] - model[c, 0:N, :])
    store(mult, mult_out.at[0])
    volume_part(2)
    volume_part(3)
    for copy in stores:
        copy.wait()


def local(phases, holograms, ctf_phase, projected, multiplier, volume, band_length, line_rows):
    any_spec = pl.BlockSpec(memory_space=pl.ANY)
    smem = pl.BlockSpec(memory_space=pltpu.SMEM)
    vmem = pl.BlockSpec(memory_space=pltpu.VMEM)
    V = pltpu.VMEM
    dma = pltpu.SemaphoreType.DMA
    table = jnp.asarray(cas_table())
    newp, update, ret = pl.pallas_call(
        main_kernel,
        out_shape=(
            jax.ShapeDtypeStruct((N, QUARTER), f32),
            jax.ShapeDtypeStruct((LINES, QUARTER), f32),
            jax.ShapeDtypeStruct((CHUNKS, 2, 4, 2, 2, BAND, CHUNK), f32),
        ),
        in_specs=[any_spec] * 6 + [vmem, smem, smem],
        out_specs=(any_spec, any_spec, any_spec),
        scratch_shapes=[
            V((N, N), bf16), V((N, N), bf16), V((N, N), bf16), V((N, N), bf16),
            V((N, N), f32), V((N, QUARTER), f32), V((N, QUARTER), f32), V((N, QUARTER), f32),
            V((4, N, QUARTER), f32),
            V((CHUNKS, 4, N, CHUNK), f32), V((CHUNKS, 2, HALF, CHUNK), f32),
            V((CHUNKS, 2, N, CHUNK), f32), V((N, QUARTER), f32),
            V((32, N), bf16), V((32, N), bf16), V((32, N), bf16), V((32, N), bf16),
            V((4, 4, 2, 8, LINES), jnp.int32), V((2, 2, 4, 2, 8, LINES), jnp.int32),
            V((2, 2, 512, LINES), bf16), V((2, 2, LINES, 512), bf16),
            V((LINES, QUARTER), f32), V((LINES, QUARTER), f32),
            V((PAD, CHUNK), f32), V((N, QUARTER), f32), V((LINES, QUARTER), f32),
            V((CHUNKS, 2, 4, 2, 2, BAND, CHUNK), f32), V((CHUNKS, 2, 8, 2, BAND, CHUNK), f32),
            V((CHUNKS, 2, 2, LINES, CHUNK), f32), V((CHUNKS, 4, LINES, CHUNK), f32),
            V((CHUNKS, 2, 2, LINES, CHUNK), f32), V((CHUNKS, 2, 8, 2, BAND, CHUNK), f32),
            dma((7,)), dma((CHUNKS, 2, 3)), dma((CHUNKS, 2, 3)),
            dma((4,)), dma((2, 2)), dma((CHUNKS, 2, 2, 8)), dma((CHUNKS, 2, 2, 8)),
            dma((CHUNKS, 2, 2)), dma((CHUNKS, 4)), dma((CHUNKS, 4)), dma((CHUNKS, 2, 2)),
            dma((CHUNKS, 2, 2, 8)), dma((CHUNKS, 2, 2, 8)), dma((2,)), dma((CHUNKS, 2, 4)),
        ],
        compiler_params=pltpu.CompilerParams(
            collective_id=0, has_side_effects=True, vmem_limit_bytes=56 * 2**20
        ),
        name="iterate",
    )(table, holograms, phases, projected, multiplier, volume, line_rows, ctf_phase, band_length)

    return pl.pallas_call(
        last_kernel,
        out_shape=(
            jax.ShapeDtypeStruct((1, N, QUARTER), f32),
            jax.ShapeDtypeStruct((4, N, QUARTER), f32),
            jax.ShapeDtypeStruct((1, N, QUARTER), f32),
        ),
        in_specs=[smem] + [any_spec] * 5,
        out_specs=(any_spec,) * 3,
        scratch_shapes=[
            V((CHUNKS, 2, 4, 2, 2, BAND, CHUNK), f32), V((N, QUARTER), f32), V((N, QUARTER), f32),
            V((4, N, QUARTER), f32), V((LINES, QUARTER), f32), V((CHUNKS, PAD, CHUNK), f32),
            dma((8,)), dma((6,)),
        ],
        compiler_params=pltpu.CompilerParams(vmem_limit_bytes=60 * 2**20),
        name="finish",
    )(band_length, ret, newp, multiplier, volume, update)


def solution(mesh):
    in_specs = (
        P("ang", None, None),
        P("grp", "ang", None, None),
        P(),
        P("ang", None, "grp"),
        P("ang", None, "grp"),
        P("ang", None, "grp"),
        P(),
        P(None, "ang", None),
    )
    out_specs = (P("ang", None, "grp"), P("ang", None, "grp"), P("ang", None, "grp"))
    return jax.shard_map(local, mesh=mesh, in_specs=in_specs, out_specs=out_specs, check_vma=False)
```

```python
import functools

import jax
import jax.numpy as jnp
import ml_dtypes
import numpy as np
from jax import lax
from jax.experimental import pallas as pl
from jax.experimental.pallas import tpu as pltpu
from jax.sharding import PartitionSpec as P

f32 = jnp.float32
bf16 = jnp.bfloat16
MESH = pl.DeviceIdType.MESH

N = 1024
QUARTER = 256
CHUNK = 128
CHUNKS = 2
SLABS = 32
BAND = 64
LINES = 256
GROUPS = 4
HALF = N // 2
PAD = N + BAND
OPP, OWN, UP, DN = range(4)

step_phase = 0.2
penalty = 0.5
step_volume = 0.004
YBLOCK = 16


def cas_tables():
    places = np.arange(N)
    angle = (places[:, None] * places[None, :] % N).astype(np.float32) * np.float32(2.0 * np.pi / N)
    table = (np.cos(angle) + np.sin(angle)).astype(ml_dtypes.bfloat16)[:HALF]
    even, odd = table[:, 0::2], table[:, 1::2]
    return np.stack([even, odd, even.T, odd.T])


def split(x):
    high = x.astype(bf16)
    return high, (x - high.astype(f32)).astype(bf16)


def static_slot(s):
    y, x, core = s // 8, s // 2 % 4, s % 2
    return (0, y, core, x // 2) if (x + y) % 2 == 0 else (1, x, core, y // 2)


def main_kernel(
    table_in, holo_in, phase_in, proj_in, mult_in, vol_in, lines_ref, ctf_ref, length_ref,
    newp_out, update_out, ret_out,
    table, holo, work_a, work_b, phase, own_phase, proj, mult, vol,
    terms, relay, arrive, grad, left_h, right_h, left_p, right_p,
    lines, lines_in, hits, hits_t, sums, first_back, target, newp, update,
    picked, inter, part_out, part_in, fresh_sums, again,
    load_sem, z_send, z_recv, l_send, l_recv, a_send, a_recv, b_send, b_recv,
    c_send, c_recv, d_send, d_recv, out_sem, own_sem,
):
    me = lax.axis_index("ang")
    z = lax.axis_index("grp")
    up = lax.rem(z + 1, GROUPS)
    dn = lax.rem(z + GROUPS - 1, GROUPS)

    y, x, core = me // 8, lax.rem(me // 2, 4), lax.rem(me, 2)
    yh, yl, xh, xl = y // 2, lax.rem(y, 2), x // 2, lax.rem(x, 2)
    kind = lax.rem(x + y, 2)
    own_high = (1 - kind) * xh + kind * yh
    own_pos = (1 - kind) * x + kind * y

    def at_place(py, px, pc):
        return py * 8 + px * 2 + pc

    loads = [
        pltpu.make_async_copy(table_in, table, load_sem.at[0]),
        pltpu.make_async_copy(holo_in.at[0, 0], holo, load_sem.at[1]),
        pltpu.make_async_copy(phase_in.at[0], phase, load_sem.at[2]),
        pltpu.make_async_copy(vol_in, vol, load_sem.at[3]),
        pltpu.make_async_copy(
            phase_in.at[0, :, pl.ds(pl.multiple_of(z * QUARTER, QUARTER), QUARTER)],
            own_phase, load_sem.at[4],
        ),
        pltpu.make_async_copy(proj_in.at[0], proj, load_sem.at[5]),
        pltpu.make_async_copy(mult_in.at[0], mult, load_sem.at[6]),
    ]
    loads[0].start()
    loads[1].start()

    barrier = pltpu.get_barrier_semaphore()

    def greet(device):
        pl.semaphore_signal(barrier, inc=1, device_id=(device, z), device_id_type=MESH)

    for d in range(4):
        for c in range(2):
            if d or c:
                greet(at_place(y, lax.rem(x + d, 4), lax.rem(core + c, 2)))
            if d:
                greet(at_place(lax.rem(y + d, 4), x, lax.rem(core + c, 2)))
    pl.semaphore_signal(barrier, inc=1, device_id=(me, up), device_id_type=MESH)
    pl.semaphore_signal(barrier, inc=1, device_id=(me, dn), device_id_type=MESH)

    column = lax.broadcasted_iota(jnp.int32, (8, N), 1)
    place = jnp.where(column < HALF, 2 * column, 2 * column - (N - 1))
    row = lax.broadcasted_iota(jnp.int32, (8, N), 0)
    folded = jnp.minimum(place, N - place).astype(f32) / N
    freq = folded * folded
    own_coef = ctf_ref[z]
    coef = jnp.where(row == 4, own_coef, 0.0)
    for dist in range(GROUPS):
        coef = jnp.where(row == dist, 2.0 * ctf_ref[dist], coef)
    theta = coef * freq
    sine, cosine = jnp.sin(theta), jnp.cos(theta)
    scale = 2.0 / (N * N)
    zeros8 = jnp.zeros((8, N), f32)

    def pack(parts, height):
        rows = jnp.concatenate(parts, axis=0)
        fill = height - rows.shape[0]
        return jnp.concatenate([rows, jnp.zeros((fill, N), f32)], axis=0).astype(bf16)

    def high(x):
        return x.astype(bf16).astype(f32)

    a_h = jnp.concatenate([sine[4:5], cosine[4:5]], axis=0)
    b_h = jnp.concatenate([cosine[4:5], sine[4:5]], axis=0) * (-scale)
    a_hi, b_hi = high(a_h), high(b_h)
    left_h[...] = pack([a_hi, a_hi, a_h - a_hi], 32)
    right_h[...] = pack([b_hi, b_h - b_hi, b_hi], 32)
    a_p = jnp.concatenate([cosine[0:4], sine[0:4]], axis=0)
    b_p = jnp.concatenate([-cosine[0:4], sine[0:4]], axis=0) * scale
    a_ph, b_ph = high(a_p), high(b_p)
    one = jnp.ones((1, N), f32)
    left_p[...] = pack([a_ph, a_ph, a_p - a_ph, one], 32)
    right_p[...] = pack([b_ph, b_p - b_ph, b_ph, one * (GROUPS * scale)], 32)

    wide = 512

    def columns(i):
        return pl.ds(pl.multiple_of(i * wide, wide), wide)

    def fold(src, dst):
        low, high_part = src[:, :HALF].astype(f32), src[:, HALF:].astype(f32)
        dst[:, :HALF] = (low + high_part).astype(bf16)
        dst[:, HALF:] = (low - high_part).astype(bf16)

    def by_table(src, dst):
        for half in range(2):
            cols = slice(half * HALF, half * HALF + HALF)
            out = jnp.dot(src[:, cols], table[half], preferred_element_type=f32)
            dst[:HALF, cols] = (out[:HALF] + out[HALF:]).astype(bf16)
            dst[HALF:, cols] = (out[:HALF] - out[HALF:]).astype(bf16)

    def filtered(src, dst, left, right):
        def body(i, _):
            cols = columns(i)
            for half in range(2):
                rows = slice(half * HALF, half * HALF + HALF)
                spectrum = jnp.dot(table[2 + half], src[rows, cols], preferred_element_type=f32)
                weight = lax.dot_general(
                    left[:, rows], right[:, cols], (((0,), (0,)), ((), ())), preferred_element_type=f32
                )
                dst[rows, cols] = (weight * spectrum).astype(bf16)
            return 0

        lax.fori_loop(0, N // wide, body, 0)

    def of_table(src, dst):
        def body(i, _):
            cols = columns(i)
            even = jnp.dot(table[0], src[:HALF, cols], preferred_element_type=f32)
            odd = jnp.dot(table[1], src[HALF:, cols], preferred_element_type=f32)
            dst[:HALF, cols] = (even + odd).astype(bf16)
            dst[HALF:, cols] = (even - odd).astype(bf16)
            return 0

        lax.fori_loop(0, N // wide, body, 0)

    loads[0].wait()
    loads[1].wait()
    for load in loads[2:]:
        load.start()
    fold(holo, work_b)
    by_table(work_b, work_a)
    filtered(work_a, work_b, left_h, right_h)
    of_table(work_b, work_a)

    near, far = lax.rem(z, 2), lax.rem(z + 1, 2)
    near_sign = (1 - 2 * (z // 2)).astype(f32)
    far_sign = (1 - 2 * (up // 2)).astype(f32)

    def all_terms(c):
        def cols(q):
            return pl.ds(pl.multiple_of(q * QUARTER + c * CHUNK, CHUNK), CHUNK)

        parts = []
        for half in range(2):
            both = jnp.concatenate([table[2 + half, :, cols(near)], table[2 + half, :, cols(far)]], axis=1)
            rows = work_a[:, half * HALF : half * HALF + HALF]
            parts.append(jnp.dot(rows, both, preferred_element_type=f32))
        even, odd = parts
        near_odd, far_odd = odd[:, :CHUNK] * near_sign, odd[:, CHUNK:] * far_sign
        terms[c, OWN] = even[:, :CHUNK] + near_odd
        terms[c, OPP] = even[:, :CHUNK] - near_odd
        terms[c, UP] = even[:, CHUNK:] + far_odd
        terms[c, DN] = even[:, CHUNK:] - far_odd

    top, bottom = pl.ds(0, HALF), pl.ds(HALF, HALF)

    def z_copy(c, way, piece):
        target_z = (up, dn)[way]
        if piece == 0:
            src, dst = terms.at[c, OPP, (top, bottom)[way]], relay.at[c, way]
        elif piece == 1:
            rows = (bottom, top)[way]
            src, dst = terms.at[c, (UP, DN)[way], rows], arrive.at[c, way, rows]
        else:
            rows = (top, bottom)[way]
            src, dst = terms.at[c, (UP, DN)[way], rows], arrive.at[c, way, rows]
        return pltpu.make_async_remote_copy(
            src_ref=src, dst_ref=dst,
            send_sem=z_send.at[c, way, piece], recv_sem=z_recv.at[c, way, piece],
            device_id=(me, target_z), device_id_type=MESH,
        )

    def start_piece(c, piece):
        z_copy(c, 0, piece).start()
        z_copy(c, 1, piece).start()

    def pass_on(c):
        z_copy(c, 0, 0).wait_recv()
        terms[c, UP, 0:HALF] += relay[c, 0]
        z_copy(c, 0, 2).start()
        z_copy(c, 1, 0).wait_recv()
        terms[c, DN, HALF:N] += relay[c, 1]
        z_copy(c, 1, 2).start()

    def tile(length, line_of):
        parts = []
        for k in range(4):
            offset = lax.broadcasted_iota(jnp.int32, (BAND, LINES), 0)
            parts.append(jnp.where((line_of(k) == offset) & (offset < length), 1.0, 0.0))
        return jnp.concatenate(parts, axis=0)

    def remote(src, dst, send, recv, device):
        return pltpu.make_async_remote_copy(
            src_ref=src, dst_ref=dst, send_sem=send, recv_sem=recv,
            device_id=(device, z), device_id_type=MESH,
        )

    def lane(way, d):
        if way == 0:
            p = lax.rem(y + d, 4)
            return p, at_place(p, x, core)
        p = lax.rem(x + d, 4)
        return p, at_place(y, p, core)

    def rows_for(ref, c, way, p):
        if way == 0:
            return ref.at[c, p // 2, lax.rem(p, 2), :, lax.rem(p, 2)]
        return ref.at[c, :, 1 - lax.rem(p, 2), p // 2, lax.rem(p, 2)]

    mine = (y, x)

    def step(way, d, dc):
        p, _ = lane(way, d)
        pc = lax.rem(core + dc, 2)
        device = at_place(p, x, pc) if way == 0 else at_place(y, p, pc)
        return p, pc, device

    others = [(d, dc) for d in (2, 1, 3) for dc in range(2)] + [(0, 1)]

    def rows_out(c, h, way, d, dc):
        p, pc, device = step(way, d, dc)
        slot = mine[way] * 2 + core
        return remote(
            picked.at[c, way, p, pc, h], inter.at[c, way, slot, h],
            a_send.at[c, h, way, p * 2 + pc], a_recv.at[c, h, way, slot], device,
        )

    def rows_in(c, h, way, d, dc):
        p, pc, device = step(way, d, dc)
        slot = p * 2 + pc
        return remote(
            picked.at[c, way, p, pc, h], inter.at[c, way, slot, h],
            a_send.at[c, h, way, slot], a_recv.at[c, h, way, slot], device,
        )

    def rows_own(c, h, way):
        return pltpu.make_async_copy(
            picked.at[c, way, mine[way], core, h],
            inter.at[c, way, mine[way] * 2 + core, h], own_sem.at[c, h, way],
        )

    def owner(way, h):
        return at_place(y, h * 2 + yl, core) if way == 0 else at_place(h * 2 + 1 - xl, x, core)

    def elsewhere(way, h):
        return pl.when(kind * 2 + own_high != way * 2 + h)

    def part_copy(c, h, way):
        pos = (x, y)[way]
        return remote(
            part_out.at[c, way, h], part_in.at[c, pos],
            b_send.at[c, way, h], b_recv.at[c, pos], owner(way, h),
        )

    def helper(j):
        pos = lax.rem(own_pos + j, 4)
        return pos, (1 - kind) * at_place(y, pos, core) + kind * at_place(pos, x, core)

    def part_arrival(c, j):
        pos, device = helper(j)
        return remote(part_out.at[c, 0, 0], part_in.at[c, pos], b_send.at[c, 0, 0], b_recv.at[c, pos], device)

    def sums_out(c, j):
        pos, device = helper(j)
        place = (c, kind, own_high)
        return remote(
            fresh_sums.at[place], fresh_sums.at[place], c_send.at[c, j], c_recv.at[place], device
        )

    def sums_in(c, h, way):
        place = (c, way, h)
        return remote(
            fresh_sums.at[place], fresh_sums.at[place], c_send.at[c, 1], c_recv.at[place], owner(way, h)
        )

    def back_out(c, h, way, d, dc):
        p, pc, device = step(way, d, dc)
        slot = p * 2 + pc
        return remote(
            again.at[c, way, slot, h], ret_out.at[c, way, mine[way], core, h],
            d_send.at[c, h, way, slot], d_recv.at[c, h, way, mine[way] * 2 + core], device,
        )

    def back_in(c, h, way, d, dc):
        p, pc, device = step(way, d, dc)
        slot = p * 2 + pc
        return remote(
            again.at[c, way, slot, h], ret_out.at[c, way, p, pc, h],
            d_send.at[c, h, way, slot], d_recv.at[c, h, way, slot], device,
        )

    def back_own(c, h, way):
        return pltpu.make_async_copy(
            again.at[c, way, mine[way] * 2 + core, h],
            ret_out.at[c, way, mine[way], core, h], own_sem.at[c, h, 2 + way],
        )

    def lines_copy(way, j):
        pos = lax.rem((x, y)[way] + j, 4)
        src = lines.at[:, pos] if way == 0 else lines.at[pos]
        device = at_place(y, pos, core) if way == 0 else at_place(pos, x, core)
        h = (xh, yh)[way]
        return remote(src, lines_in.at[way, h], l_send.at[j], l_recv.at[way, h], device)

    def lines_arrival(way, h):
        src = lines.at[:, 0] if way == 0 else lines.at[0]
        return remote(src, lines_in.at[way, h], l_send.at[1], l_recv.at[way, h], owner(way, h))

    def send_lines():
        for a in range(SLABS):
            four = lines_ref[a]
            line = jnp.concatenate([four[v : v + 1] for v in range(4)], axis=1)
            lines[a // 8, a // 2 % 4, a % 2] = jnp.broadcast_to(line, (8, LINES))
        for way in range(2):

            @pl.when(kind == way)
            def _():
                for j in range(1, 4):
                    lines_copy(way, j).start()
                if way == 0:
                    lines_in[0, own_high] = lines[:, x]
                else:
                    lines_in[1, own_high] = lines[y]

    def own_counts():
        own_length = length_ref[me]

        def body(g, total):
            def line_of(k):
                a = g * 4 + k
                return lines[a // 8, lax.rem(a // 2, 4), lax.rem(a, 2)][0:1]

            one = tile(own_length, line_of)
            return total + jnp.dot(
                jnp.transpose(one).astype(bf16), one.astype(bf16), preferred_element_type=f32
            )

        total = lax.fori_loop(0, 8, body, jnp.zeros((LINES, LINES), f32))
        hi, lo = split(sums[...])
        both = jnp.dot(total.astype(bf16), jnp.concatenate([hi, lo], axis=1), preferred_element_type=f32)
        first_back[...] = both[:, :QUARTER] + both[:, QUARTER:]

    def build_hits():
        for way in range(2):
            for h in range(2):

                @elsewhere(way, h)
                def _():
                    lines_arrival(way, h).wait_recv()

            def body(n, _):
                h, g = n // 2, lax.rem(n, 2)
                length = length_ref[owner(way, h)]

                def line_of(k):
                    return lines_in[way, h, g * 2 + k // 2, k % 2][0:1]

                one = tile(length, line_of)
                at = pl.ds(pl.multiple_of(g * 256, 256), 256)
                hits[way, h, at, :] = one.astype(bf16)
                hits_t[way, h, :, at] = jnp.transpose(one).astype(bf16)
                return 0

            lax.fori_loop(0, 4, body, 0)

    def send_rows(c, h):
        for d, dc in others:
            for way in range(2):
                rows_out(c, h, way, d, dc).start()
        for way in range(2):
            rows_own(c, h, way).start()

    def send_parts(c, h):
        for way in range(2):
            for d, dc in others:
                rows_in(c, h, way, d, dc).wait_recv()
            rows_own(c, h, way).wait()
            rows = inter[c, way, :, pl.ds(h, 1)].reshape(512, CHUNK)
            hi, lo = split(rows)
            both = jnp.dot(hits_t[way, h], jnp.concatenate([hi, lo], axis=1), preferred_element_type=f32)
            part_out[c, way, h] = both[:, :CHUNK] + both[:, CHUNK:]

            @elsewhere(way, h)
            def _():
                part_copy(c, h, way).start()

    def send_sums(c):
        cols = pl.ds(c * CHUNK, CHUNK)
        for j in range(1, 4):
            part_arrival(c, j).wait_recv()
        total = part_out[c, kind, own_high]
        for j in range(1, 4):
            total = total + part_in[c, lax.rem(own_pos + j, 4)]
        back = first_back[:, cols] - total
        update[:, cols] = back
        fresh_sums[c, kind, own_high] = sums[:, cols] - (step_volume * YBLOCK) * back
        for j in range(1, 4):
            sums_out(c, j).start()

    def send_back(c, h):
        for way in range(2):

            @elsewhere(way, h)
            def _():
                sums_in(c, h, way).wait_recv()

            hi, lo = split(fresh_sums[c, way, h])
            both = jnp.dot(hits[way, h], jnp.concatenate([hi, lo], axis=1), preferred_element_type=f32)
            again[c, way, :, pl.ds(h, 1)] = (both[:, :CHUNK] + both[:, CHUNK:]).reshape(8, 1, BAND, CHUNK)
            for d, dc in others:
                back_out(c, h, way, d, dc).start()
            back_own(c, h, way).start()

    def wait_all(c):
        for h in range(2):
            for way in range(2):
                for d, dc in others:
                    back_in(c, h, way, d, dc).wait_recv()
                    if h == 1:
                        rows_out(c, h, way, d, dc).wait_send()
                    back_out(c, h, way, d, dc).wait_send()
                back_own(c, h, way).wait()

                @elsewhere(way, h)
                def _():
                    part_copy(c, h, way).wait_send()

        for j in range(1, 4):
            sums_out(c, j).wait_send()

    def new_phases(c):
        cols = pl.ds(c * CHUNK, CHUNK)
        for way in range(2):
            z_copy(c, way, 1).wait_recv()
            z_copy(c, way, 2).wait_recv()
        gradient = grad[:, cols] + terms[c, OWN] + arrive[c, 0] + arrive[c, 1]
        own = own_phase[:, cols]
        dual = mult[:, cols]
        fresh = own - step_phase * (gradient + penalty * (own - proj[:, cols]) + dual)
        newp[:, cols] = fresh
        target[0:N, :] = fresh + dual / penalty

        for h in range(2):
            start = 0
            for s in range(SLABS):
                slot = static_slot(s)
                if slot[3] == h:
                    picked[(c, *slot)] = target[pl.ds(start, BAND), :]
                start = start + length_ref[s]
            send_rows(c, h)
            if h == 0:
                for d, dc in others:
                    for way in range(2):
                        rows_out(c, 0, way, d, dc).wait_send()

    all_terms(0)
    pl.semaphore_wait(barrier, 15)
    start_piece(0, 0)
    all_terms(1)
    send_lines()
    start_piece(0, 1)

    loads[2].wait()
    fold(phase, work_b)
    by_table(work_b, work_a)
    pass_on(0)
    filtered(work_a, work_b, left_p, right_p)
    near_cols = pl.ds(pl.multiple_of(near * QUARTER, QUARTER), QUARTER)
    even = jnp.dot(work_b[:, :HALF], table[2, :, near_cols], preferred_element_type=f32)
    odd = jnp.dot(work_b[:, HALF:], table[3, :, near_cols], preferred_element_type=f32)
    part = (even + odd * near_sign).astype(bf16)
    start_piece(1, 0)
    even = jnp.dot(table[0], part[:HALF], preferred_element_type=f32)
    odd = jnp.dot(table[1], part[HALF:], preferred_element_type=f32)
    grad[:HALF, :] = even + odd
    grad[HALF:, :] = even - odd

    loads[3].wait()
    for v in range(4):
        sums[pl.ds(v * 64, 64), :] = jnp.sum(vol[v].reshape(64, YBLOCK, QUARTER), axis=1)
    for load in loads[4:]:
        load.wait()
    start_piece(1, 1)
    target[N:PAD, :] = jnp.zeros((BAND, CHUNK), f32)

    new_phases(0)
    own_counts()
    pass_on(1)
    build_hits()
    send_parts(0,0)
    send_parts(0,1)
    new_phases(1)
    save_phases = pltpu.make_async_copy(newp, newp_out, out_sem.at[0])
    save_phases.start()
    send_sums(0)
    send_parts(1,0)
    send_parts(1,1)
    send_back(0,0)
    send_back(0,1)
    send_sums(1)
    save_update = pltpu.make_async_copy(update, update_out, out_sem.at[1])
    save_update.start()
    send_back(1,0)
    send_back(1,1)

    for way in range(2):

        @pl.when(kind == way)
        def _():
            for j in range(1, 4):
                lines_copy(way, j).wait_send()

    for c in range(CHUNKS):
        for way in range(2):
            for piece in range(3):
                z_copy(c, way, piece).wait_send()
        wait_all(c)
    save_phases.wait()
    save_update.wait()


def last_kernel(
    length_ref, ret_in, newp_in, mult_in, vol_in, update_in, newp_out, vol_out, mult_out,
    ret, newp, mult, vol, update, model, sem_in, sem_out,
):
    load_update = pltpu.make_async_copy(update_in, update, sem_in.at[0])
    load_vol = [pltpu.make_async_copy(vol_in.at[v], vol.at[v], sem_in.at[1 + v]) for v in range(4)]
    load_ret = pltpu.make_async_copy(ret_in, ret, sem_in.at[5])
    load_newp = pltpu.make_async_copy(newp_in, newp, sem_in.at[6])
    load_mult = pltpu.make_async_copy(mult_in.at[0], mult, sem_in.at[7])
    for load in (load_update, load_newp, load_vol[0], load_ret, load_vol[1], load_mult, load_vol[2], load_vol[3]):
        load.start()

    stores = []

    def store(src, dst):
        copy = pltpu.make_async_copy(src, dst, sem_out.at[len(stores)])
        copy.start()
        stores.append(copy)

    def volume_part(v):
        load_vol[v].wait()
        change = step_volume * update[v * 64 : v * 64 + 64, :]
        shaped = jnp.broadcast_to(change[:, None, :], (64, YBLOCK, QUARTER)).reshape(N, QUARTER)
        vol[v] = vol[v] - shaped
        store(vol.at[v], vol_out.at[v])

    load_update.wait()
    load_newp.wait()
    store(newp, newp_out.at[0])
    volume_part(0)
    load_ret.wait()
    start = 0
    for s in range(SLABS):
        for c in range(CHUNKS):
            model[c, pl.ds(start, BAND), :] = ret[(c, *static_slot(s))]
        start = start + length_ref[s]
    volume_part(1)
    load_mult.wait()
    for c in range(CHUNKS):
        cols = slice(c * CHUNK, (c + 1) * CHUNK)
        mult[:, cols] = mult[:, cols] + penalty * (newp[:, cols] - model[c, 0:N, :])
    store(mult, mult_out.at[0])
    volume_part(2)
    volume_part(3)
    for copy in stores:
        copy.wait()


def local(phases, holograms, ctf_phase, projected, multiplier, volume, band_length, line_rows):
    any_spec = pl.BlockSpec(memory_space=pl.ANY)
    smem = pl.BlockSpec(memory_space=pltpu.SMEM)
    vmem = pl.BlockSpec(memory_space=pltpu.VMEM)
    V = pltpu.VMEM
    dma = pltpu.SemaphoreType.DMA
    table = jnp.asarray(cas_tables())
    newp, update, ret = pl.pallas_call(
        main_kernel,
        out_shape=(
            jax.ShapeDtypeStruct((N, QUARTER), f32),
            jax.ShapeDtypeStruct((LINES, QUARTER), f32),
            jax.ShapeDtypeStruct((CHUNKS, 2, 4, 2, 2, BAND, CHUNK), f32),
        ),
        in_specs=[any_spec] * 6 + [vmem, smem, smem],
        out_specs=(any_spec, any_spec, any_spec),
        scratch_shapes=[
            V((4, HALF, HALF), bf16), V((N, N), bf16), V((N, N), bf16), V((N, N), bf16),
            V((N, N), f32), V((N, QUARTER), f32), V((N, QUARTER), f32), V((N, QUARTER), f32),
            V((4, N, QUARTER), f32),
            V((CHUNKS, 4, N, CHUNK), f32), V((CHUNKS, 2, HALF, CHUNK), f32),
            V((CHUNKS, 2, N, CHUNK), f32), V((N, QUARTER), f32),
            V((32, N), bf16), V((32, N), bf16), V((32, N), bf16), V((32, N), bf16),
            V((4, 4, 2, 8, LINES), jnp.int32), V((2, 2, 4, 2, 8, LINES), jnp.int32),
            V((2, 2, 512, LINES), bf16), V((2, 2, LINES, 512), bf16),
            V((LINES, QUARTER), f32), V((LINES, QUARTER), f32),
            V((PAD, CHUNK), f32), V((N, QUARTER), f32), V((LINES, QUARTER), f32),
            V((CHUNKS, 2, 4, 2, 2, BAND, CHUNK), f32), V((CHUNKS, 2, 8, 2, BAND, CHUNK), f32),
            V((CHUNKS, 2, 2, LINES, CHUNK), f32), V((CHUNKS, 4, LINES, CHUNK), f32),
            V((CHUNKS, 2, 2, LINES, CHUNK), f32), V((CHUNKS, 2, 8, 2, BAND, CHUNK), f32),
            dma((7,)), dma((CHUNKS, 2, 3)), dma((CHUNKS, 2, 3)),
            dma((4,)), dma((2, 2)), dma((CHUNKS, 2, 2, 8)), dma((CHUNKS, 2, 2, 8)),
            dma((CHUNKS, 2, 2)), dma((CHUNKS, 4)), dma((CHUNKS, 4)), dma((CHUNKS, 2, 2)),
            dma((CHUNKS, 2, 2, 8)), dma((CHUNKS, 2, 2, 8)), dma((2,)), dma((CHUNKS, 2, 4)),
        ],
        compiler_params=pltpu.CompilerParams(
            collective_id=0, has_side_effects=True, vmem_limit_bytes=56 * 2**20
        ),
        name="iterate",
    )(table, holograms, phases, projected, multiplier, volume, line_rows, ctf_phase, band_length)

    return pl.pallas_call(
        last_kernel,
        out_shape=(
            jax.ShapeDtypeStruct((1, N, QUARTER), f32),
            jax.ShapeDtypeStruct((4, N, QUARTER), f32),
            jax.ShapeDtypeStruct((1, N, QUARTER), f32),
        ),
        in_specs=[smem] + [any_spec] * 5,
        out_specs=(any_spec,) * 3,
        scratch_shapes=[
            V((CHUNKS, 2, 4, 2, 2, BAND, CHUNK), f32), V((N, QUARTER), f32), V((N, QUARTER), f32),
            V((4, N, QUARTER), f32), V((LINES, QUARTER), f32), V((CHUNKS, PAD, CHUNK), f32),
            dma((8,)), dma((6,)),
        ],
        compiler_params=pltpu.CompilerParams(vmem_limit_bytes=60 * 2**20),
        name="finish",
    )(band_length, ret, newp, multiplier, volume, update)


def solution(mesh):
    in_specs = (
        P("ang", None, None),
        P("grp", "ang", None, None),
        P(),
        P("ang", None, "grp"),
        P("ang", None, "grp"),
        P("ang", None, "grp"),
        P(),
        P(None, "ang", None),
    )
    out_specs = (P("ang", None, "grp"), P("ang", None, "grp"), P("ang", None, "grp"))
    return jax.shard_map(local, mesh=mesh, in_specs=in_specs, out_specs=out_specs, check_vma=False)
```

```python
import functools

import jax
import jax.numpy as jnp
import ml_dtypes
import numpy as np
from jax import lax
from jax.experimental import pallas as pl
from jax.experimental.pallas import tpu as pltpu
from jax.sharding import PartitionSpec as P

f32 = jnp.float32
bf16 = jnp.bfloat16
MESH = pl.DeviceIdType.MESH

N = 1024
QUARTER = 256
CHUNK = 128
CHUNKS = 2
SLABS = 32
BAND = 64
LINES = 256
GROUPS = 4
HALF = N // 2
PAD = N + BAND
OPP, OWN, UP, DN = range(4)

step_phase = 0.2
penalty = 0.5
step_volume = 0.004
YBLOCK = 16


def cas_tables():
    places = np.arange(N)
    angle = (places[:, None] * places[None, :] % N).astype(np.float32) * np.float32(2.0 * np.pi / N)
    table = (np.cos(angle) + np.sin(angle)).astype(ml_dtypes.bfloat16)[:HALF]
    even, odd = table[:, 0::2], table[:, 1::2]
    return np.stack([even, odd, even.T, odd.T])


def split(x):
    high = x.astype(bf16)
    return high, (x - high.astype(f32)).astype(bf16)


def static_slot(s):
    y, x, core = s // 8, s // 2 % 4, s % 2
    return (0, y, core, x // 2) if (x + y) % 2 == 0 else (1, x, core, y // 2)


def main_kernel(
    table_in, holo_in, phase_in, proj_in, mult_in, vol_in, lines_ref, ctf_ref, length_ref,
    newp_out, update_out, ret_out,
    table, holo, work_a, work_b, phase, own_phase, proj, mult, vol,
    terms, relay, arrive, grad, left_h, right_h, left_p, right_p,
    lines, lines_in, hits, hits_t, sums, first_back, target, newp, update,
    picked, inter, part_out, part_in, fresh_sums, again,
    load_sem, z_send, z_recv, l_send, l_recv, a_send, a_recv, b_send, b_recv,
    c_send, c_recv, d_send, d_recv, out_sem, own_sem,
):
    me = lax.axis_index("ang")
    z = lax.axis_index("grp")
    up = lax.rem(z + 1, GROUPS)
    dn = lax.rem(z + GROUPS - 1, GROUPS)

    y, x, core = me // 8, lax.rem(me // 2, 4), lax.rem(me, 2)
    yh, yl, xh, xl = y // 2, lax.rem(y, 2), x // 2, lax.rem(x, 2)
    kind = lax.rem(x + y, 2)
    own_high = (1 - kind) * xh + kind * yh
    own_pos = (1 - kind) * x + kind * y

    def at_place(py, px, pc):
        return py * 8 + px * 2 + pc

    loads = [
        pltpu.make_async_copy(table_in, table, load_sem.at[0]),
        pltpu.make_async_copy(holo_in.at[0, 0], holo, load_sem.at[1]),
        pltpu.make_async_copy(phase_in.at[0], phase, load_sem.at[2]),
        pltpu.make_async_copy(vol_in, vol, load_sem.at[3]),
        pltpu.make_async_copy(
            phase_in.at[0, :, pl.ds(pl.multiple_of(z * QUARTER, QUARTER), QUARTER)],
            own_phase, load_sem.at[4],
        ),
        pltpu.make_async_copy(proj_in.at[0], proj, load_sem.at[5]),
        pltpu.make_async_copy(mult_in.at[0], mult, load_sem.at[6]),
    ]
    loads[0].start()
    loads[1].start()

    barrier = pltpu.get_barrier_semaphore()

    def greet(device):
        pl.semaphore_signal(barrier, inc=1, device_id=(device, z), device_id_type=MESH)

    for d in range(4):
        for c in range(2):
            if d or c:
                greet(at_place(y, lax.rem(x + d, 4), lax.rem(core + c, 2)))
            if d:
                greet(at_place(lax.rem(y + d, 4), x, lax.rem(core + c, 2)))
    pl.semaphore_signal(barrier, inc=1, device_id=(me, up), device_id_type=MESH)
    pl.semaphore_signal(barrier, inc=1, device_id=(me, dn), device_id_type=MESH)

    column = lax.broadcasted_iota(jnp.int32, (8, N), 1)
    place = jnp.where(column < HALF, 2 * column, 2 * column - (N - 1))
    row = lax.broadcasted_iota(jnp.int32, (8, N), 0)
    folded = jnp.minimum(place, N - place).astype(f32) / N
    freq = folded * folded
    own_coef = ctf_ref[z]
    coef = jnp.where(row == 4, own_coef, 0.0)
    for dist in range(GROUPS):
        coef = jnp.where(row == dist, 2.0 * ctf_ref[dist], coef)
    theta = coef * freq
    sine, cosine = jnp.sin(theta), jnp.cos(theta)
    scale = 2.0 / (N * N)
    zeros8 = jnp.zeros((8, N), f32)

    def pack(parts, height):
        rows = jnp.concatenate(parts, axis=0)
        fill = height - rows.shape[0]
        return jnp.concatenate([rows, jnp.zeros((fill, N), f32)], axis=0).astype(bf16)

    def high(x):
        return x.astype(bf16).astype(f32)

    a_h = jnp.concatenate([sine[4:5], cosine[4:5]], axis=0)
    b_h = jnp.concatenate([cosine[4:5], sine[4:5]], axis=0) * (-scale)
    a_hi, b_hi = high(a_h), high(b_h)
    left_h[...] = pack([a_hi, a_hi, a_h - a_hi], 32)
    right_h[...] = pack([b_hi, b_h - b_hi, b_hi], 32)
    a_p = jnp.concatenate([cosine[0:4], sine[0:4]], axis=0)
    b_p = jnp.concatenate([-cosine[0:4], sine[0:4]], axis=0) * scale
    a_ph, b_ph = high(a_p), high(b_p)
    one = jnp.ones((1, N), f32)
    left_p[...] = pack([a_ph, a_ph, a_p - a_ph, one], 32)
    right_p[...] = pack([b_ph, b_p - b_ph, b_ph, one * (GROUPS * scale)], 32)

    wide = 512

    def columns(i):
        return pl.ds(pl.multiple_of(i * wide, wide), wide)

    def fold(src, dst):
        low, high_part = src[:, :HALF].astype(f32), src[:, HALF:].astype(f32)
        dst[:, :HALF] = (low + high_part).astype(bf16)
        dst[:, HALF:] = (low - high_part).astype(bf16)

    def by_table(src, dst):
        for half in range(2):
            cols = slice(half * HALF, half * HALF + HALF)
            out = jnp.dot(src[:, cols], table[half], preferred_element_type=f32)
            dst[:HALF, cols] = (out[:HALF] + out[HALF:]).astype(bf16)
            dst[HALF:, cols] = (out[:HALF] - out[HALF:]).astype(bf16)

    def filtered(src, dst, left, right):
        def body(i, _):
            cols = columns(i)
            for half in range(2):
                rows = slice(half * HALF, half * HALF + HALF)
                spectrum = jnp.dot(table[2 + half], src[rows, cols], preferred_element_type=f32)
                weight = lax.dot_general(
                    left[:, rows], right[:, cols], (((0,), (0,)), ((), ())), preferred_element_type=f32
                )
                dst[rows, cols] = (weight * spectrum).astype(bf16)
            return 0

        lax.fori_loop(0, N // wide, body, 0)

    def of_table(src, dst):
        def body(i, _):
            cols = columns(i)
            even = jnp.dot(table[0], src[:HALF, cols], preferred_element_type=f32)
            odd = jnp.dot(table[1], src[HALF:, cols], preferred_element_type=f32)
            dst[:HALF, cols] = (even + odd).astype(bf16)
            dst[HALF:, cols] = (even - odd).astype(bf16)
            return 0

        lax.fori_loop(0, N // wide, body, 0)

    loads[0].wait()
    loads[1].wait()
    for load in loads[2:]:
        load.start()
    fold(holo, work_b)
    by_table(work_b, work_a)
    filtered(work_a, work_b, left_h, right_h)
    of_table(work_b, work_a)

    near, far = lax.rem(z, 2), lax.rem(z + 1, 2)
    near_sign = (1 - 2 * (z // 2)).astype(f32)
    far_sign = (1 - 2 * (up // 2)).astype(f32)

    def all_terms(c):
        def cols(q):
            return pl.ds(pl.multiple_of(q * QUARTER + c * CHUNK, CHUNK), CHUNK)

        parts = []
        for half in range(2):
            both = jnp.concatenate([table[2 + half, :, cols(near)], table[2 + half, :, cols(far)]], axis=1)
            rows = work_a[:, half * HALF : half * HALF + HALF]
            parts.append(jnp.dot(rows, both, preferred_element_type=f32))
        even, odd = parts
        near_odd, far_odd = odd[:, :CHUNK] * near_sign, odd[:, CHUNK:] * far_sign
        terms[c, OWN] = even[:, :CHUNK] + near_odd
        terms[c, OPP] = even[:, :CHUNK] - near_odd
        terms[c, UP] = even[:, CHUNK:] + far_odd
        terms[c, DN] = even[:, CHUNK:] - far_odd

    top, bottom = pl.ds(0, HALF), pl.ds(HALF, HALF)

    def z_copy(c, way, piece):
        target_z = (up, dn)[way]
        if piece == 0:
            src, dst = terms.at[c, OPP, (top, bottom)[way]], relay.at[c, way]
        elif piece == 1:
            rows = (bottom, top)[way]
            src, dst = terms.at[c, (UP, DN)[way], rows], arrive.at[c, way, rows]
        else:
            rows = (top, bottom)[way]
            src, dst = terms.at[c, (UP, DN)[way], rows], arrive.at[c, way, rows]
        return pltpu.make_async_remote_copy(
            src_ref=src, dst_ref=dst,
            send_sem=z_send.at[c, way, piece], recv_sem=z_recv.at[c, way, piece],
            device_id=(me, target_z), device_id_type=MESH,
        )

    def start_piece(c, piece):
        z_copy(c, 0, piece).start()
        z_copy(c, 1, piece).start()

    def pass_on(c):
        z_copy(c, 0, 0).wait_recv()
        terms[c, UP, 0:HALF] += relay[c, 0]
        z_copy(c, 0, 2).start()
        z_copy(c, 1, 0).wait_recv()
        terms[c, DN, HALF:N] += relay[c, 1]
        z_copy(c, 1, 2).start()

    def tile(length, line_of):
        parts = []
        for k in range(4):
            offset = lax.broadcasted_iota(jnp.int32, (BAND, LINES), 0)
            parts.append(jnp.where((line_of(k) == offset) & (offset < length), 1.0, 0.0))
        return jnp.concatenate(parts, axis=0)

    def remote(src, dst, send, recv, device):
        return pltpu.make_async_remote_copy(
            src_ref=src, dst_ref=dst, send_sem=send, recv_sem=recv,
            device_id=(device, z), device_id_type=MESH,
        )

    def lane(way, d):
        if way == 0:
            p = lax.rem(y + d, 4)
            return p, at_place(p, x, core)
        p = lax.rem(x + d, 4)
        return p, at_place(y, p, core)

    def rows_for(ref, c, way, p):
        if way == 0:
            return ref.at[c, p // 2, lax.rem(p, 2), :, lax.rem(p, 2)]
        return ref.at[c, :, 1 - lax.rem(p, 2), p // 2, lax.rem(p, 2)]

    mine = (y, x)

    def step(way, d, dc):
        p, _ = lane(way, d)
        pc = lax.rem(core + dc, 2)
        device = at_place(p, x, pc) if way == 0 else at_place(y, p, pc)
        return p, pc, device

    others = [(d, dc) for d in (2, 1, 3) for dc in range(2)] + [(0, 1)]

    def rows_out(c, h, way, d, dc):
        p, pc, device = step(way, d, dc)
        slot = mine[way] * 2 + core
        return remote(
            picked.at[c, way, p, pc, h], inter.at[c, way, slot, h],
            a_send.at[c, h, way, p * 2 + pc], a_recv.at[c, h, way, slot], device,
        )

    def rows_in(c, h, way, d, dc):
        p, pc, device = step(way, d, dc)
        slot = p * 2 + pc
        return remote(
            picked.at[c, way, p, pc, h], inter.at[c, way, slot, h],
            a_send.at[c, h, way, slot], a_recv.at[c, h, way, slot], device,
        )

    def rows_own(c, h, way):
        return pltpu.make_async_copy(
            picked.at[c, way, mine[way], core, h],
            inter.at[c, way, mine[way] * 2 + core, h], own_sem.at[c, h, way],
        )

    def owner(way, h):
        return at_place(y, h * 2 + yl, core) if way == 0 else at_place(h * 2 + 1 - xl, x, core)

    def elsewhere(way, h):
        return pl.when(kind * 2 + own_high != way * 2 + h)

    def part_copy(c, h, way):
        pos = (x, y)[way]
        return remote(
            part_out.at[c, way, h], part_in.at[c, pos],
            b_send.at[c, way, h], b_recv.at[c, pos], owner(way, h),
        )

    def helper(j):
        pos = lax.rem(own_pos + j, 4)
        return pos, (1 - kind) * at_place(y, pos, core) + kind * at_place(pos, x, core)

    def part_arrival(c, j):
        pos, device = helper(j)
        return remote(part_out.at[c, 0, 0], part_in.at[c, pos], b_send.at[c, 0, 0], b_recv.at[c, pos], device)

    def sums_out(c, j):
        pos, device = helper(j)
        place = (c, kind, own_high)
        return remote(
            fresh_sums.at[place], fresh_sums.at[place], c_send.at[c, j], c_recv.at[place], device
        )

    def sums_in(c, h, way):
        place = (c, way, h)
        return remote(
            fresh_sums.at[place], fresh_sums.at[place], c_send.at[c, 1], c_recv.at[place], owner(way, h)
        )

    def back_out(c, h, way, d, dc):
        p, pc, device = step(way, d, dc)
        slot = p * 2 + pc
        return remote(
            again.at[c, way, slot, h], ret_out.at[c, way, mine[way], core, h],
            d_send.at[c, h, way, slot], d_recv.at[c, h, way, mine[way] * 2 + core], device,
        )

    def back_in(c, h, way, d, dc):
        p, pc, device = step(way, d, dc)
        slot = p * 2 + pc
        return remote(
            again.at[c, way, slot, h], ret_out.at[c, way, p, pc, h],
            d_send.at[c, h, way, slot], d_recv.at[c, h, way, slot], device,
        )

    def back_own(c, h, way):
        return pltpu.make_async_copy(
            again.at[c, way, mine[way] * 2 + core, h],
            ret_out.at[c, way, mine[way], core, h], own_sem.at[c, h, 2 + way],
        )

    def lines_copy(way, j):
        pos = lax.rem((x, y)[way] + j, 4)
        src = lines.at[:, pos] if way == 0 else lines.at[pos]
        device = at_place(y, pos, core) if way == 0 else at_place(pos, x, core)
        h = (xh, yh)[way]
        return remote(src, lines_in.at[way, h], l_send.at[j], l_recv.at[way, h], device)

    def lines_arrival(way, h):
        src = lines.at[:, 0] if way == 0 else lines.at[0]
        return remote(src, lines_in.at[way, h], l_send.at[1], l_recv.at[way, h], owner(way, h))

    def send_lines():
        for a in range(SLABS):
            four = lines_ref[a]
            line = jnp.concatenate([four[v : v + 1] for v in range(4)], axis=1)
            lines[a // 8, a // 2 % 4, a % 2] = jnp.broadcast_to(line, (8, LINES))
        for way in range(2):

            @pl.when(kind == way)
            def _():
                for j in range(1, 4):
                    lines_copy(way, j).start()
                if way == 0:
                    lines_in[0, own_high] = lines[:, x]
                else:
                    lines_in[1, own_high] = lines[y]

    def own_counts():
        own_length = length_ref[me]

        def body(g, total):
            def line_of(k):
                a = g * 4 + k
                return lines[a // 8, lax.rem(a // 2, 4), lax.rem(a, 2)][0:1]

            one = tile(own_length, line_of)
            return total + jnp.dot(
                jnp.transpose(one).astype(bf16), one.astype(bf16), preferred_element_type=f32
            )

        total = lax.fori_loop(0, 8, body, jnp.zeros((LINES, LINES), f32))
        hi, lo = split(sums[...])
        both = jnp.dot(total.astype(bf16), jnp.concatenate([hi, lo], axis=1), preferred_element_type=f32)
        first_back[...] = both[:, :QUARTER] + both[:, QUARTER:]

    def build_hits():
        for way in range(2):
            for h in range(2):

                @elsewhere(way, h)
                def _():
                    lines_arrival(way, h).wait_recv()

            def body(n, _):
                h, g = n // 2, lax.rem(n, 2)
                length = length_ref[owner(way, h)]

                def line_of(k):
                    return lines_in[way, h, g * 2 + k // 2, k % 2][0:1]

                one = tile(length, line_of)
                at = pl.ds(pl.multiple_of(g * 256, 256), 256)
                hits[way, h, at, :] = one.astype(bf16)
                hits_t[way, h, :, at] = jnp.transpose(one).astype(bf16)
                return 0

            lax.fori_loop(0, 4, body, 0)

    def send_rows(c, h):
        for d, dc in others:
            for way in range(2):
                rows_out(c, h, way, d, dc).start()
        for way in range(2):
            rows_own(c, h, way).start()

    def send_parts(c, h):
        for way in range(2):
            for d, dc in others:
                rows_in(c, h, way, d, dc).wait_recv()
            rows_own(c, h, way).wait()
            rows = inter[c, way, :, pl.ds(h, 1)].reshape(512, CHUNK)
            hi, lo = split(rows)
            both = jnp.dot(hits_t[way, h], jnp.concatenate([hi, lo], axis=1), preferred_element_type=f32)
            part_out[c, way, h] = both[:, :CHUNK] + both[:, CHUNK:]

            @elsewhere(way, h)
            def _():
                part_copy(c, h, way).start()

    def send_sums(c):
        cols = pl.ds(c * CHUNK, CHUNK)
        for j in range(1, 4):
            part_arrival(c, j).wait_recv()
        total = part_out[c, kind, own_high]
        for j in range(1, 4):
            total = total + part_in[c, lax.rem(own_pos + j, 4)]
        back = first_back[:, cols] - total
        fresh_sums[c, kind, own_high] = sums[:, cols] - (step_volume * YBLOCK) * back
        for j in range(1, 4):
            sums_out(c, j).start()
        update[:, cols] = back

    def send_back(c, h):
        for way in range(2):

            @elsewhere(way, h)
            def _():
                sums_in(c, h, way).wait_recv()

            hi, lo = split(fresh_sums[c, way, h])
            both = jnp.dot(hits[way, h], jnp.concatenate([hi, lo], axis=1), preferred_element_type=f32)
            again[c, way, :, pl.ds(h, 1)] = (both[:, :CHUNK] + both[:, CHUNK:]).reshape(8, 1, BAND, CHUNK)
            for d, dc in others:
                back_out(c, h, way, d, dc).start()
            back_own(c, h, way).start()

    def wait_all(c):
        for h in range(2):
            for way in range(2):
                for d, dc in others:
                    back_in(c, h, way, d, dc).wait_recv()
                    if h == 1:
                        rows_out(c, h, way, d, dc).wait_send()
                    back_out(c, h, way, d, dc).wait_send()
                back_own(c, h, way).wait()

                @elsewhere(way, h)
                def _():
                    part_copy(c, h, way).wait_send()

        for j in range(1, 4):
            sums_out(c, j).wait_send()

    def new_phases(c):
        cols = pl.ds(c * CHUNK, CHUNK)
        for way in range(2):
            z_copy(c, way, 1).wait_recv()
            z_copy(c, way, 2).wait_recv()
        gradient = grad[:, cols] + terms[c, OWN] + arrive[c, 0] + arrive[c, 1]
        own = own_phase[:, cols]
        dual = mult[:, cols]
        fresh = own - step_phase * (gradient + penalty * (own - proj[:, cols]) + dual)
        newp[:, cols] = fresh
        target[0:N, :] = fresh + dual / penalty

        for h in range(2):
            start = 0
            for s in range(SLABS):
                slot = static_slot(s)
                if slot[3] == h:
                    picked[(c, *slot)] = target[pl.ds(start, BAND), :]
                start = start + length_ref[s]
            send_rows(c, h)
            if h == 0:
                for d, dc in others:
                    for way in range(2):
                        rows_out(c, 0, way, d, dc).wait_send()

    all_terms(0)
    pl.semaphore_wait(barrier, 15)
    start_piece(0, 0)
    all_terms(1)
    send_lines()
    start_piece(0, 1)

    loads[2].wait()
    fold(phase, work_b)
    by_table(work_b, work_a)
    pass_on(0)
    filtered(work_a, work_b, left_p, right_p)
    near_cols = pl.ds(pl.multiple_of(near * QUARTER, QUARTER), QUARTER)
    even = jnp.dot(work_b[:, :HALF], table[2, :, near_cols], preferred_element_type=f32)
    odd = jnp.dot(work_b[:, HALF:], table[3, :, near_cols], preferred_element_type=f32)
    part = (even + odd * near_sign).astype(bf16)
    start_piece(1, 0)
    even = jnp.dot(table[0], part[:HALF], preferred_element_type=f32)
    odd = jnp.dot(table[1], part[HALF:], preferred_element_type=f32)
    grad[:HALF, :] = even + odd
    grad[HALF:, :] = even - odd

    loads[3].wait()
    for v in range(4):
        sums[pl.ds(v * 64, 64), :] = jnp.sum(vol[v].reshape(64, YBLOCK, QUARTER), axis=1)
    for load in loads[4:]:
        load.wait()
    start_piece(1, 1)
    target[N:PAD, :] = jnp.zeros((BAND, CHUNK), f32)

    new_phases(0)
    own_counts()
    pass_on(1)
    build_hits()
    send_parts(0,0)
    send_parts(0,1)
    new_phases(1)
    save_phases = pltpu.make_async_copy(newp, newp_out, out_sem.at[0])
    save_phases.start()
    send_sums(0)
    send_parts(1,0)
    send_parts(1,1)
    send_back(0,0)
    send_back(0,1)
    send_sums(1)
    save_update = pltpu.make_async_copy(update, update_out, out_sem.at[1])
    save_update.start()
    send_back(1,0)
    send_back(1,1)

    for way in range(2):

        @pl.when(kind == way)
        def _():
            for j in range(1, 4):
                lines_copy(way, j).wait_send()

    for c in range(CHUNKS):
        for way in range(2):
            for piece in range(3):
                z_copy(c, way, piece).wait_send()
        wait_all(c)
    save_phases.wait()
    save_update.wait()


def last_kernel(
    length_ref, ret_in, newp_in, mult_in, vol_in, update_in, newp_out, vol_out, mult_out,
    ret, newp, mult, vol, update, model, sem_in, sem_out,
):
    load_update = pltpu.make_async_copy(update_in, update, sem_in.at[0])
    load_vol = [pltpu.make_async_copy(vol_in.at[v], vol.at[v], sem_in.at[1 + v]) for v in range(4)]
    load_ret = pltpu.make_async_copy(ret_in, ret, sem_in.at[5])
    load_newp = pltpu.make_async_copy(newp_in, newp, sem_in.at[6])
    load_mult = pltpu.make_async_copy(mult_in.at[0], mult, sem_in.at[7])
    for load in (load_update, load_newp, load_vol[0], load_ret, load_vol[1], load_mult, load_vol[2], load_vol[3]):
        load.start()

    stores = []

    def store(src, dst):
        copy = pltpu.make_async_copy(src, dst, sem_out.at[len(stores)])
        copy.start()
        stores.append(copy)

    def volume_part(v):
        load_vol[v].wait()
        change = step_volume * update[v * 64 : v * 64 + 64, :]
        shaped = jnp.broadcast_to(change[:, None, :], (64, YBLOCK, QUARTER)).reshape(N, QUARTER)
        vol[v] = vol[v] - shaped
        store(vol.at[v], vol_out.at[v])

    load_update.wait()
    load_newp.wait()
    store(newp, newp_out.at[0])
    volume_part(0)
    load_ret.wait()
    start = 0
    for s in range(SLABS):
        for c in range(CHUNKS):
            model[c, pl.ds(start, BAND), :] = ret[(c, *static_slot(s))]
        start = start + length_ref[s]
    volume_part(1)
    load_mult.wait()
    for c in range(CHUNKS):
        cols = slice(c * CHUNK, (c + 1) * CHUNK)
        mult[:, cols] = mult[:, cols] + penalty * (newp[:, cols] - model[c, 0:N, :])
    store(mult, mult_out.at[0])
    volume_part(2)
    volume_part(3)
    for copy in stores:
        copy.wait()


def local(phases, holograms, ctf_phase, projected, multiplier, volume, band_length, line_rows):
    any_spec = pl.BlockSpec(memory_space=pl.ANY)
    smem = pl.BlockSpec(memory_space=pltpu.SMEM)
    vmem = pl.BlockSpec(memory_space=pltpu.VMEM)
    V = pltpu.VMEM
    dma = pltpu.SemaphoreType.DMA
    table = jnp.asarray(cas_tables())
    newp, update, ret = pl.pallas_call(
        main_kernel,
        out_shape=(
            jax.ShapeDtypeStruct((N, QUARTER), f32),
            jax.ShapeDtypeStruct((LINES, QUARTER), f32),
            jax.ShapeDtypeStruct((CHUNKS, 2, 4, 2, 2, BAND, CHUNK), f32),
        ),
        in_specs=[any_spec] * 6 + [vmem, smem, smem],
        out_specs=(any_spec, any_spec, any_spec),
        scratch_shapes=[
            V((4, HALF, HALF), bf16), V((N, N), bf16), V((N, N), bf16), V((N, N), bf16),
            V((N, N), f32), V((N, QUARTER), f32), V((N, QUARTER), f32), V((N, QUARTER), f32),
            V((4, N, QUARTER), f32),
            V((CHUNKS, 4, N, CHUNK), f32), V((CHUNKS, 2, HALF, CHUNK), f32),
            V((CHUNKS, 2, N, CHUNK), f32), V((N, QUARTER), f32),
            V((32, N), bf16), V((32, N), bf16), V((32, N), bf16), V((32, N), bf16),
            V((4, 4, 2, 8, LINES), jnp.int32), V((2, 2, 4, 2, 8, LINES), jnp.int32),
            V((2, 2, 512, LINES), bf16), V((2, 2, LINES, 512), bf16),
            V((LINES, QUARTER), f32), V((LINES, QUARTER), f32),
            V((PAD, CHUNK), f32), V((N, QUARTER), f32), V((LINES, QUARTER), f32),
            V((CHUNKS, 2, 4, 2, 2, BAND, CHUNK), f32), V((CHUNKS, 2, 8, 2, BAND, CHUNK), f32),
            V((CHUNKS, 2, 2, LINES, CHUNK), f32), V((CHUNKS, 4, LINES, CHUNK), f32),
            V((CHUNKS, 2, 2, LINES, CHUNK), f32), V((CHUNKS, 2, 8, 2, BAND, CHUNK), f32),
            dma((7,)), dma((CHUNKS, 2, 3)), dma((CHUNKS, 2, 3)),
            dma((4,)), dma((2, 2)), dma((CHUNKS, 2, 2, 8)), dma((CHUNKS, 2, 2, 8)),
            dma((CHUNKS, 2, 2)), dma((CHUNKS, 4)), dma((CHUNKS, 4)), dma((CHUNKS, 2, 2)),
            dma((CHUNKS, 2, 2, 8)), dma((CHUNKS, 2, 2, 8)), dma((2,)), dma((CHUNKS, 2, 4)),
        ],
        compiler_params=pltpu.CompilerParams(
            collective_id=0, has_side_effects=True, vmem_limit_bytes=56 * 2**20
        ),
        name="iterate",
    )(table, holograms, phases, projected, multiplier, volume, line_rows, ctf_phase, band_length)

    return pl.pallas_call(
        last_kernel,
        out_shape=(
            jax.ShapeDtypeStruct((1, N, QUARTER), f32),
            jax.ShapeDtypeStruct((4, N, QUARTER), f32),
            jax.ShapeDtypeStruct((1, N, QUARTER), f32),
        ),
        in_specs=[smem] + [any_spec] * 5,
        out_specs=(any_spec,) * 3,
        scratch_shapes=[
            V((CHUNKS, 2, 4, 2, 2, BAND, CHUNK), f32), V((N, QUARTER), f32), V((N, QUARTER), f32),
            V((4, N, QUARTER), f32), V((LINES, QUARTER), f32), V((CHUNKS, PAD, CHUNK), f32),
            dma((8,)), dma((6,)),
        ],
        compiler_params=pltpu.CompilerParams(vmem_limit_bytes=60 * 2**20),
        name="finish",
    )(band_length, ret, newp, multiplier, volume, update)


def solution(mesh):
    in_specs = (
        P("ang", None, None),
        P("grp", "ang", None, None),
        P(),
        P("ang", None, "grp"),
        P("ang", None, "grp"),
        P("ang", None, "grp"),
        P(),
        P(None, "ang", None),
    )
    out_specs = (P("ang", None, "grp"), P("ang", None, "grp"), P("ang", None, "grp"))
    return jax.shard_map(local, mesh=mesh, in_specs=in_specs, out_specs=out_specs, check_vma=False)
```
